32 devices in a mesh: rep: 2 (over x), blk: 16 (over z, y, core).
Axes of the slice: x: 2, y: 2, z: 4, core: 2. Of those that a mesh axis runs over, the one named last changes fastest.
Arguments:
- amplitudes: bfloat16 [96, 1024, 1024], P('blk', 'rep'), may hold values from -6 to 6
- integrals: bfloat16 [96, 1024, 1024], P('blk', 'rep'), may hold values from -0.0017089844 to 0.0017089844
- fock_matrix: bfloat16 [1024, 1024], P('blk'), may hold values from -0.5 to 0.5
- hole_ladder: float32 [96, 96], P('blk'), may hold values from -1.75 to 1.75
- virt_irrep: int32 [1024], replicated, may hold values from 0 to 7
- occ_irrep: int32 [128], replicated, may hold values from 0 to 7
- pair_index: int32 [96, 2], replicated, may hold values from 0 to 127
- eps_occ: float32 [128], replicated, may hold values from -2 to -0.5
- eps_virt: float32 [1024], replicated, may hold values from 0.3 to 3
Outputs:
- update: bfloat16 [96, 1024, 1024], P('blk', 'rep')
The draws below stay inside these ranges and needn't reach their ends.
All inputs are finite; a program needn't handle non-finite values.
Results may differ from the reference program's by a relative error of at most 0.0075.
Values may be sent and summed in bfloat16 or wider, within the bound.
No kernel may reach another device: no remote copies, remote signals or barrier semaphores. Data moves between devices by JAX's collectives and lax.ppermute only.
A program may use at most 128 MiB of HBM per device.

```python
import jax
import jax.numpy as jnp
from jax import lax

V = 1024
O = 128
P_SIZE = 96


def set_ends(array, stream_key, low, largest):
    longest = array.shape.index(max(array.shape))
    spots = []
    for shift in (0, 1):
        where = [jax.random.randint(jax.random.fold_in(stream_key, axis), (), 0, length) for axis, length in enumerate(array.shape)]
        where[longest] = (where[longest] + shift) % array.shape[longest]
        spots.append(tuple(where))
    return array.at[spots[0]].set(low).at[spots[1]].set(largest)


def level_of(rng, shape, shards, smallest, largest):
    def one(dim, shards_of):
        heights = jax.random.uniform(jax.random.fold_in(jax.random.fold_in(rng, 6), dim), (shards_of,), jnp.float32, smallest / len(shards), largest / len(shards))
        return jnp.repeat(jnp.exp(heights), shape[dim] // shards_of).reshape((-1,) + (1,) * (len(shape) - dim - 1))

    gain = one(*shards[0])
    for cut in shards[1:]:
        gain = gain * one(*cut)
    return gain


def normal_values(stream_key, shape, scale, bound, cuts=(), dtype=jnp.bfloat16):
    entries = jax.random.normal(stream_key, shape, jnp.float32) * scale
    if len(cuts) > 0:
        entries = level_of(stream_key, shape, cuts, -0.22, 0.18) * entries
    return jnp.clip(entries, min=-bound, max=bound).astype(dtype)


def setup_inputs(seed: int = 0) -> dict:
    keys = jax.random.split(jax.random.key(seed), 10)
    amplitudes = normal_values(keys[0], (P_SIZE, V, V), 1.0, 6.0, ((0, 16), (1, 2)))
    integrals = normal_values(keys[1], (P_SIZE, V, V), (V * V * P_SIZE // 8) ** -0.5, 0.0017089844, ((0, 16), (1, 2)))
    fock_matrix = normal_values(keys[2], (V, V), (V // 8) ** -0.5, 0.5, ((0, 16),))
    hole_ladder = normal_values(keys[3], (P_SIZE, P_SIZE), (P_SIZE // 8) ** -0.5, 1.75, ((0, 16),), jnp.float32)
    virt_irrep = set_ends(jax.random.randint(keys[4], (V,), 0, 8), jax.random.fold_in(keys[4], 1), 0, 7).astype(jnp.int32)
    occ_irrep = set_ends(jax.random.randint(keys[5], (O,), 0, 8), jax.random.fold_in(keys[5], 1), 0, 7).astype(jnp.int32)
    pair_index = set_ends(jax.random.randint(keys[6], (P_SIZE, 2), 0, O), jax.random.fold_in(keys[6], 1), 0, O - 1).astype(jnp.int32)
    eps_occ = jnp.clip(jax.random.uniform(keys[7], (O,), jnp.float32, -2.0, -0.5), -2.0, -0.5)
    eps_virt = jnp.clip(jax.random.uniform(keys[8], (V,), jnp.float32, 0.3, 3.0), 0.3, 3.0)
    return {"amplitudes": amplitudes, "integrals": integrals, "fock_matrix": fock_matrix, "hole_ladder": hole_ladder, "virt_irrep": virt_irrep, "occ_irrep": occ_irrep, "pair_index": pair_index, "eps_occ": eps_occ, "eps_virt": eps_virt}


def reference(amplitudes, integrals, fock_matrix, hole_ladder, virt_irrep, occ_irrep, pair_index, eps_occ, eps_virt):
    same_virt = virt_irrep[:, None] == virt_irrep[None, :]
    fock_kept = jnp.where(same_virt, fock_matrix, jnp.zeros_like(fock_matrix))
    amp_rows = amplitudes.reshape(P_SIZE, V * V)
    int_rows = integrals.reshape(P_SIZE, V * V)
    pair_sums = jnp.dot(amp_rows, int_rows.T, preferred_element_type=jnp.float32)
    pair_irrep = jnp.bitwise_xor(occ_irrep[pair_index[:, 0]], occ_irrep[pair_index[:, 1]])
    same_pair = pair_irrep[:, None] == pair_irrep[None, :]
    ladder = jnp.where(same_pair, hole_ladder + pair_sums, jnp.zeros_like(pair_sums)).astype(jnp.bfloat16)
    pair_energy = eps_occ[pair_index[:, 0]] + eps_occ[pair_index[:, 1]]

    def one_pair(index):
        fock_term = jnp.dot(amplitudes[index], fock_kept.T, preferred_element_type=jnp.float32).astype(jnp.bfloat16)
        ladder_term = jnp.dot(ladder[index][None, :], amp_rows, preferred_element_type=jnp.float32)
        ladder_term = ladder_term.reshape(V, V).astype(jnp.bfloat16)
        denom = pair_energy[index] - eps_virt[:, None] - eps_virt[None, :]
        total = fock_term.astype(jnp.float32) + ladder_term.astype(jnp.float32)
        return (total / denom).astype(jnp.bfloat16)

    return lax.map(one_pair, jnp.arange(P_SIZE))
```

```python
import jax
import jax.numpy as jnp
from jax import lax
from jax.sharding import PartitionSpec as P


def table_lookup(index_col, table):
    iota_rows = jnp.arange(table.shape[0], dtype=jnp.int32)
    equal = index_col[:, None] == iota_rows[None, :]
    return jnp.sum(jnp.where(equal, table[None, :], jnp.zeros_like(table)[None, :]), axis=1)


def shards(
    amplitudes,
    integrals,
    fock_matrix,
    hole_ladder,
    virt_irrep,
    occ_irrep,
    pair_index,
    eps_occ,
    eps_virt,
):
    pair_dev = amplitudes.shape[0]
    virt_rows = amplitudes.shape[1]
    virt_all = amplitudes.shape[2]
    blk_count = lax.axis_size("blk")
    rows_each = virt_rows // blk_count
    pair_total = pair_dev * blk_count
    blk_id = lax.axis_index("blk")
    rep_id = lax.axis_index("rep")
    piece = lax.all_gather(fock_matrix, "blk", axis=0, tiled=True)
    kept = jnp.where(virt_irrep[:, None] == virt_irrep[None, :], piece, jnp.zeros_like(piece))
    fock_term = jnp.einsum(
        "pac,bc->pab", amplitudes, kept, preferred_element_type=jnp.float32
    ).astype(jnp.bfloat16)
    amp_virt, int_virt = (
        lax.all_to_all(amplitudes, "blk", split_axis=1, concat_axis=0, tiled=True),
        lax.all_to_all(integrals, "blk", split_axis=1, concat_axis=0, tiled=True),
    )
    amp_flat = amp_virt.reshape(pair_total, rows_each * virt_all)
    int_flat = int_virt.reshape(pair_total, rows_each * virt_all)
    partial_sums = jnp.dot(amp_flat, int_flat.T, preferred_element_type=jnp.float32)
    pair_irrep = jnp.bitwise_xor(
        table_lookup(pair_index[:, 0], occ_irrep), table_lookup(pair_index[:, 1], occ_irrep)
    )
    pair_energy = table_lookup(pair_index[:, 0], eps_occ) + table_lookup(pair_index[:, 1], eps_occ)
    summed = lax.psum(partial_sums, ("rep", "blk"))
    hole_all = lax.all_gather(hole_ladder, "blk", axis=0, tiled=True)
    same_pair = pair_irrep[:, None] == pair_irrep[None, :]
    ladder = jnp.where(same_pair, hole_all + summed, jnp.zeros_like(summed)).astype(jnp.bfloat16)
    ladder_virt = jnp.dot(ladder, amp_flat, preferred_element_type=jnp.float32)
    ladder_virt = ladder_virt.reshape(pair_total, rows_each, virt_all).astype(jnp.bfloat16)
    ladder_term = lax.all_to_all(ladder_virt, "blk", split_axis=0, concat_axis=1, tiled=True)
    row_energy = lax.dynamic_slice_in_dim(eps_virt, rep_id * virt_rows, virt_rows)
    own_energy = lax.dynamic_slice_in_dim(pair_energy, blk_id * pair_dev, pair_dev)
    denom = own_energy[:, None, None] - row_energy[None, :, None] - eps_virt[None, None, :]
    total = fock_term.astype(jnp.float32) + ladder_term.astype(jnp.float32)
    return (total / denom).astype(jnp.bfloat16)


def solution(mesh):
    return jax.shard_map(
        shards,
        mesh=mesh,
        in_specs=(
            P("blk", "rep", None),
            P("blk", "rep", None),
            P("blk", None),
            P("blk", None),
            P(),
            P(),
            P(),
            P(),
            P(),
        ),
        out_specs=P("blk", "rep", None),
        check_vma=False,
    )
```

```python
import functools

import jax
import jax.numpy as jnp
from jax import lax
from jax.experimental import pallas as pl
from jax.experimental.pallas import tpu as pltpu
from jax.sharding import PartitionSpec as P

PLANES = 4
INNER = 4
CHUNK = 16
CHUNKS = 8
WIDE = 5
LANES = 128
VMEM_BYTES = 56 * 1024 * 1024


def table_lookup(index_col, table):
    iota_rows = jnp.arange(table.shape[0], dtype=jnp.int32)
    equal = index_col[:, None] == iota_rows[None, :]
    return jnp.sum(jnp.where(equal, table[None, :], jnp.zeros_like(table)[None, :]), axis=1)


def spread_plan(
    amplitudes,
    integrals,
    fock_matrix,
    hole_ladder,
    virt_irrep,
    occ_irrep,
    pair_index,
    eps_occ,
    eps_virt,
):
    pair_dev = amplitudes.shape[0]
    virt_rows = amplitudes.shape[1]
    virt_all = amplitudes.shape[2]
    blk_count = lax.axis_size("blk")
    rows_each = virt_rows // blk_count
    pair_total = pair_dev * blk_count
    blk_id = lax.axis_index("blk")
    rep_id = lax.axis_index("rep")
    piece = lax.all_gather(fock_matrix, "blk", axis=0, tiled=True)
    kept = jnp.where(virt_irrep[:, None] == virt_irrep[None, :], piece, jnp.zeros_like(piece))
    fock_term = jnp.einsum(
        "pac,bc->pab", amplitudes, kept, preferred_element_type=jnp.float32
    ).astype(jnp.bfloat16)
    amp_virt, int_virt = (
        lax.all_to_all(amplitudes, "blk", split_axis=1, concat_axis=0, tiled=True),
        lax.all_to_all(integrals, "blk", split_axis=1, concat_axis=0, tiled=True),
    )
    amp_flat = amp_virt.reshape(pair_total, rows_each * virt_all)
    int_flat = int_virt.reshape(pair_total, rows_each * virt_all)
    partial_sums = jnp.dot(amp_flat, int_flat.T, preferred_element_type=jnp.float32)
    pair_irrep = jnp.bitwise_xor(
        table_lookup(pair_index[:, 0], occ_irrep), table_lookup(pair_index[:, 1], occ_irrep)
    )
    pair_energy = table_lookup(pair_index[:, 0], eps_occ) + table_lookup(pair_index[:, 1], eps_occ)
    summed = lax.psum(partial_sums, ("rep", "blk"))
    hole_all = lax.all_gather(hole_ladder, "blk", axis=0, tiled=True)
    same_pair = pair_irrep[:, None] == pair_irrep[None, :]
    ladder = jnp.where(same_pair, hole_all + summed, jnp.zeros_like(summed)).astype(jnp.bfloat16)
    ladder_virt = jnp.dot(ladder, amp_flat, preferred_element_type=jnp.float32)
    ladder_virt = ladder_virt.reshape(pair_total, rows_each, virt_all).astype(jnp.bfloat16)
    ladder_term = lax.all_to_all(ladder_virt, "blk", split_axis=0, concat_axis=1, tiled=True)
    row_energy = lax.dynamic_slice_in_dim(eps_virt, rep_id * virt_rows, virt_rows)
    own_energy = lax.dynamic_slice_in_dim(pair_energy, blk_id * pair_dev, pair_dev)
    denom = own_energy[:, None, None] - row_energy[None, :, None] - eps_virt[None, None, :]
    total = fock_term.astype(jnp.float32) + ladder_term.astype(jnp.float32)
    return (total / denom).astype(jnp.bfloat16)


def plane_perm(step, first, last):
    return [
        (plane * INNER + at, (plane + step) * INNER + at)
        for plane in range(first, last + 1)
        for at in range(INNER)
    ]


def inner_perm(flip, planes=range(PLANES)):
    return [(p * INNER + at, p * INNER + (at ^ flip)) for p in planes for at in range(INNER)]


def outward_perm(flip):
    return [
        (p * INNER + at, q * INNER + (at ^ flip)) for p, q in ((1, 0), (2, 3)) for at in range(INNER)
    ]


def sixth(index):
    return sum((index >= edge).astype(jnp.int32) for edge in (6, 12, 18))


def pair_at(index, me, pair_dev):
    group = sixth(index)
    return pair_dev * (me ^ group) + index - pair_dev * group


def place_sources(plane, own, plus, minus, chunk):
    wide = chunk < WIDE
    table = {
        1: {0: plus[chunk], 1: own, 2: minus[chunk], 3: minus[CHUNKS + chunk]},
        2: {0: plus[CHUNKS + chunk], 1: plus[chunk], 2: own, 3: minus[chunk]},
    }
    if wide:
        table[0] = {0: own, 1: minus[chunk], 2: minus[WIDE + chunk], 3: minus[2 * WIDE + chunk]}
        table[3] = {0: plus[2 * WIDE + chunk], 1: plus[WIDE + chunk], 2: plus[chunk], 3: own}
    return table


def source_steps(chunk):
    steps = [chunk, CHUNKS + chunk]
    if chunk < WIDE:
        steps += [WIDE + chunk, 2 * WIDE + chunk]
    return sorted(set(steps))


def chunk_refs(chunk, own, plus, minus):
    steps = source_steps(chunk)
    return [own[chunk]] + [plus[s] for s in steps] + [minus[s] for s in steps]


def ref_table(chunk, refs):
    steps = source_steps(chunk)
    count = len(steps)
    plus = dict(zip(steps, refs[1 : 1 + count]))
    minus = dict(zip(steps, refs[1 + count : 1 + 2 * count]))
    return place_sources(None, refs[0], plus, minus, chunk)


def here():
    blk = lax.axis_index("blk")
    return lax.div(blk, INNER), lax.rem(blk, INNER)


def blocked_sum(left, right):
    rows, depth = left.shape[0], left.shape[1]
    cols = right.shape[0]
    gram = lax.dot_general(
        left.reshape(rows * depth, -1),
        right.reshape(cols * depth, -1),
        (((1,), (1,)), ((), ())),
        preferred_element_type=jnp.float32,
    )
    row_id = lax.broadcasted_iota(jnp.int32, gram.shape, 0)
    col_id = lax.broadcasted_iota(jnp.int32, gram.shape, 1)
    same = (row_id & (depth - 1)) == (col_id & (depth - 1))
    return jnp.where(same, gram, 0.0).reshape(rows, depth, cols * depth).sum(axis=1)


def exact_dot(left, right):
    return jnp.dot(left, right, preferred_element_type=jnp.float32, precision=lax.Precision.HIGHEST)


def pad_rows(array):
    extra = LANES - array.shape[0]
    return jnp.concatenate([array, jnp.zeros((extra, array.shape[1]), array.dtype)], axis=0)


def pair_kernel(chunk, last, pair_dev, *refs):
    wide = chunk < WIDE
    count = 1 + 2 * len(source_steps(chunk))
    table = ref_table(chunk, refs[:count])
    refs = refs[count:]
    if wide:
        (int_own,), refs = refs[:1], refs[1:]
        int_near = None
    else:
        (int_own, int_plus, int_minus), refs = refs[:3], refs[3:]
        int_near = {1: int_plus, 2: int_minus}
    acc_in, refs = refs[0], refs[1:]
    if last:
        hole_ref, refs = refs[0], refs[1:]
    out_ref, amp, ints, total, sems = refs
    plane, me = here()
    rows = amp.shape[1]
    total[...] = acc_in[...]
    for z, sources in table.items():

        @pl.when(plane == z)
        def _():
            copies = [pltpu.make_async_copy(int_own, ints.at[0], sems.at[PLANES])]
            if int_near is not None:
                copies.append(pltpu.make_async_copy(int_near[z], ints.at[1], sems.at[PLANES + 1]))
            for p in range(PLANES):
                copies.append(pltpu.make_async_copy(sources[p], amp.at[p], sems.at[p]))
            for copy in copies:
                copy.start()
            for copy in copies:
                copy.wait()
            for p in range(PLANES):
                for side in range(1 if wide else 2):
                    total[side, p * rows : (p + 1) * rows] += blocked_sum(amp[p], ints[side])

    if not last:
        out_ref[...] = total[...]
        return
    lanes = total.shape[2]
    placed = hole_ref[...]
    summed = jnp.zeros((total.shape[1], LANES), jnp.float32)
    near = jnp.where(plane < 2, 0, PLANES - 1)
    row_id = lax.broadcasted_iota(jnp.int32, (lanes, LANES), 0) // CHUNK
    col_id = lax.broadcasted_iota(jnp.int32, (lanes, LANES), 1)
    pair_id = pair_at(row_id, me, pair_dev)
    for side, at in ((0, plane), (1, near)):
        chosen = (col_id == pair_id + at * rows).astype(jnp.float32)
        summed += exact_dot(total[side], chosen)
    out_id = lax.broadcasted_iota(jnp.int32, (total.shape[1], LANES), 0)
    in_id = lax.broadcasted_iota(jnp.int32, (total.shape[1], LANES), 1)
    in_plane = sum((in_id >= p * rows).astype(jnp.int32) for p in range(1, PLANES))
    in_pair = pair_at(in_id - in_plane * rows, me, pair_dev) + in_plane * rows
    chosen = (out_id == in_pair).astype(jnp.float32)
    out_ref[...] = placed + exact_dot(chosen, pad_rows(summed))


def add_pair_sums(chunk, own, plus, minus, int_own, acc, hole, pair_dev):
    last = hole is not None
    rows, depth, width = own[chunk].shape
    operands = chunk_refs(chunk, own, plus, minus) + [int_own[chunk]]
    if chunk >= WIDE:
        operands += [plus[CHUNKS + chunk - WIDE], minus[CHUNKS + chunk - WIDE]]
    far = len(operands)
    operands.append(acc)
    if last:
        operands.append(hole)
    shape = (PLANES * rows, LANES) if last else acc.shape
    flops = 2 * PLANES * (rows * depth) ** 2 * width * (1 if chunk < WIDE else 2)
    return pl.pallas_call(
        functools.partial(pair_kernel, chunk, last, pair_dev),
        out_shape=jax.ShapeDtypeStruct(shape, jnp.float32),
        in_specs=[pl.BlockSpec(memory_space=pl.ANY)] * far
        + [pl.BlockSpec(memory_space=pltpu.VMEM)] * (len(operands) - far),
        out_specs=pl.BlockSpec(memory_space=pltpu.VMEM),
        scratch_shapes=[
            pltpu.VMEM((PLANES, rows, depth, width), jnp.bfloat16),
            pltpu.VMEM((2, rows, depth, width), jnp.bfloat16),
            pltpu.VMEM(acc.shape, jnp.float32),
            pltpu.SemaphoreType.DMA((PLANES + 2,)),
        ],
        compiler_params=pltpu.CompilerParams(vmem_limit_bytes=VMEM_BYTES),
        cost_estimate=pl.CostEstimate(flops=flops, bytes_accessed=5 * rows * depth * width * 2, transcendentals=0),
        name=f"pair_sums_{chunk}",
    )(*operands)


def ladder_kernel(chunks, pair_dev, *refs):
    wide = chunks[0] < WIDE
    tables = []
    for chunk in chunks:
        count = 1 + 2 * len(source_steps(chunk))
        tables.append(ref_table(chunk, refs[:count]))
        refs = refs[count:]
    sum_ref, mask_ref = refs[:2]
    outs = refs[2 : 2 + (INNER if wide else 2 * INNER)]
    amp, spread, sems = refs[2 + len(outs) :]
    plane, me = here()
    rows, depth, width = amp.shape[2:]
    block = rows * depth

    def work(z):
        copies = [
            [pltpu.make_async_copy(table[z][p], amp.at[n, p], sems.at[n, p]) for p in range(PLANES)]
            for n, table in enumerate(tables)
        ]
        for group in copies:
            for copy in group:
                copy.start()
        ladder = jnp.where(mask_ref[...] > 0, sum_ref[...], 0.0).astype(jnp.bfloat16)
        ladder = pad_rows(ladder)
        near = 0 if z < 2 else PLANES - 1
        col = lax.broadcasted_iota(jnp.int32, (LANES, PLANES * block), 1) // depth
        col_plane = sum((col >= p * rows).astype(jnp.int32) for p in range(1, PLANES))
        col_pair = pair_at(col - col_plane * rows, me, pair_dev) + col_plane * rows
        col_one = (lax.broadcasted_iota(jnp.int32, col.shape, 0) == col_pair).astype(jnp.bfloat16)
        row = lax.broadcasted_iota(jnp.int32, (block, LANES), 0) // depth
        row_pair = pair_at(row, me, pair_dev)
        for side, at in enumerate((z,) if wide else (z, near)):
            row_one = (lax.broadcasted_iota(jnp.int32, row.shape, 1) == row_pair + at * rows).astype(jnp.bfloat16)
            picked = jnp.dot(row_one, ladder, preferred_element_type=jnp.float32).astype(jnp.bfloat16)
            full = jnp.dot(picked, col_one, preferred_element_type=jnp.float32)
            left = lax.broadcasted_iota(jnp.int32, full.shape, 0) & (depth - 1)
            right = lax.broadcasted_iota(jnp.int32, full.shape, 1) & (depth - 1)
            spread[side] = jnp.where(left == right, full, 0.0).astype(jnp.bfloat16)
        for n, group in enumerate(copies):
            for copy in group:
                copy.wait()
            columns = amp[n].reshape(PLANES * block, width)
            for side in range(1 if wide else 2):
                term = jnp.dot(spread[side], columns, preferred_element_type=jnp.float32).astype(jnp.bfloat16)
                term = term.reshape(INNER, pair_dev, depth, width)
                for flip in range(INNER):
                    outs[side * INNER + flip][:, n * depth : (n + 1) * depth, :] = term[flip]

    for z in tables[0]:
        pl.when(plane == z)(functools.partial(work, z))


def ladder_terms(chunks, own, plus, minus, summed, mask, pair_dev):
    rows, depth, width = own[chunks[0]].shape
    wide = chunks[0] < WIDE
    operands = [ref for chunk in chunks for ref in chunk_refs(chunk, own, plus, minus)]
    far = len(operands)
    operands += [summed, mask]
    sides = 1 if wide else 2
    block = rows * depth
    return pl.pallas_call(
        functools.partial(ladder_kernel, chunks, pair_dev),
        out_shape=[jax.ShapeDtypeStruct((pair_dev, len(chunks) * depth, width), jnp.bfloat16)] * (sides * INNER),
        in_specs=[pl.BlockSpec(memory_space=pl.ANY)] * far + [pl.BlockSpec(memory_space=pltpu.VMEM)] * 2,
        out_specs=[pl.BlockSpec(memory_space=pltpu.VMEM)] * (sides * INNER),
        scratch_shapes=[
            pltpu.VMEM((len(chunks), PLANES, rows, depth, width), jnp.bfloat16),
            pltpu.VMEM((sides, block, PLANES * block), jnp.bfloat16),
            pltpu.SemaphoreType.DMA((len(chunks), PLANES)),
        ],
        compiler_params=pltpu.CompilerParams(vmem_limit_bytes=VMEM_BYTES),
        cost_estimate=pl.CostEstimate(
            flops=2 * PLANES * block * block * width * sides * len(chunks),
            bytes_accessed=(PLANES + sides) * block * width * 2 * len(chunks),
            transcendentals=0,
        ),
        name=f"ladder_{chunks[0]}",
    )(*operands)


def scale_kernel(pick, base_ref, energy_ref, *refs):
    if pick:
        fock, inside, outside, row_energy, col_energy, out = refs
        plane, _ = here()
        middle = (plane == 1) | (plane == 2)
    else:
        fock, inside, row_energy, col_energy, out = refs
    for p in range(fock.shape[0]):
        ladder = inside[p]
        if pick:
            ladder = jnp.where(middle, ladder, outside[p])
        denom = energy_ref[p] - row_energy[...] - col_energy[...]
        total = fock[p].astype(jnp.float32) + ladder.astype(jnp.float32)
        out[p] = (total / denom).astype(out.dtype)


def add_and_scale(buffer, pieces, base, own_energy, row_energy, col_energy):
    pair_dev, _, width = buffer.shape
    steps = pieces[0].shape[1] // CHUNK
    place = pl.BlockSpec((pair_dev, CHUNK, width), lambda i, b, e: (0, b[0] + i, 0))
    piece = pl.BlockSpec((pair_dev, CHUNK, width), lambda i, b, e: (0, i, 0))
    return pl.pallas_call(
        functools.partial(scale_kernel, len(pieces) > 1),
        out_shape=jax.ShapeDtypeStruct(buffer.shape, buffer.dtype),
        grid_spec=pltpu.PrefetchScalarGridSpec(
            num_scalar_prefetch=2,
            grid=(steps,),
            in_specs=[place]
            + [piece] * len(pieces)
            + [
                pl.BlockSpec((CHUNK, 1), lambda i, b, e: (b[0] + i, 0)),
                pl.BlockSpec((1, width), lambda i, b, e: (0, 0)),
            ],
            out_specs=place,
        ),
        input_output_aliases={2: 0},
        compiler_params=pltpu.CompilerParams(vmem_limit_bytes=VMEM_BYTES),
        cost_estimate=pl.CostEstimate(
            flops=5 * steps * CHUNK * pair_dev * width,
            bytes_accessed=(2 + len(pieces)) * steps * CHUNK * pair_dev * width * 2,
            transcendentals=0,
        ),
        name="add_and_scale",
    )(base, own_energy, buffer, *pieces, row_energy, col_energy)


def exchange_inner(array, groups, me):
    found = {}
    for first, end in groups:
        parts = []
        for flip in range(INNER):
            part = lax.dynamic_slice_in_dim(array[:, :, first:end], me ^ flip, 1, axis=1)[:, 0]
            if flip:
                part = lax.ppermute(part, "blk", inner_perm(flip))
            parts.append(part)
        for chunk in range(first, end):
            found[chunk] = jnp.concatenate([part[:, chunk - first] for part in parts], axis=0)
    return found


def line_plan(
    amplitudes,
    integrals,
    fock_matrix,
    hole_ladder,
    virt_irrep,
    occ_irrep,
    pair_index,
    eps_occ,
    eps_virt,
):
    pair_dev, virt_rows, virt_all = amplitudes.shape
    pair_total = pair_dev * PLANES * INNER
    blk_id = lax.axis_index("blk")
    rep_id = lax.axis_index("rep")
    plane, me = here()
    split = (pair_dev, INNER, CHUNKS, CHUNK, virt_all)
    own = exchange_inner(amplitudes.reshape(split), ((0, 1), (1, 3), (3, CHUNKS)), me)
    int_own = exchange_inner(integrals.reshape(split), ((WIDE, CHUNKS), (0, WIDE)), me)

    piece = lax.all_gather(fock_matrix, "blk", axis=0, tiled=True)
    kept = jnp.where(virt_irrep[:, None] == virt_irrep[None, :], piece, jnp.zeros_like(piece))
    fock_term = jnp.einsum(
        "pac,bc->pab", amplitudes, kept, preferred_element_type=jnp.float32
    ).astype(jnp.bfloat16)

    narrow = CHUNKS - WIDE
    got = {1: {}, -1: {}}
    for step in range(2 * CHUNKS):
        for way in (1, -1):
            far = plane if way == 1 else PLANES - 1 - plane
            have = got[way]
            first, last = 0, 2
            if step < WIDE:
                send = own[step]
            elif step < CHUNKS:
                send = jnp.where(far == 2, have[step - WIDE], own[step])
            else:
                send = have[step - CHUNKS]
                if step < 2 * WIDE:
                    send = jnp.where(far == 2, have[step - WIDE], send)
                elif step < 3 * WIDE:
                    send = jnp.where(far == 2, have[step - 2 * WIDE + CHUNKS], send)
                else:
                    last = 1
                if step < CHUNKS + narrow:
                    send = jnp.where(far == 0, int_own[WIDE + step - CHUNKS], send)
                else:
                    first = 1
            if way == 1:
                perm = plane_perm(1, first, last)
            else:
                perm = plane_perm(-1, PLANES - 1 - last, PLANES - 1 - first)
            have[step] = lax.ppermute(send, "blk", perm)
    plus, minus = got[1], got[-1]

    hole = jnp.zeros((pair_total, LANES), jnp.float32)
    hole_rows = jnp.pad(hole_ladder, ((0, 0), (0, LANES - pair_total)))
    hole = lax.dynamic_update_slice_in_dim(hole, hole_rows, blk_id * pair_dev, axis=0)
    hole = jnp.where(rep_id == 0, hole, jnp.zeros_like(hole))
    acc = jnp.zeros((2, pair_total, pair_dev * INNER * CHUNK), jnp.float32)
    order = sorted(range(CHUNKS), key=lambda c: (2 * WIDE if c < WIDE else CHUNKS) + c)
    for chunk in order:
        extra = hole if chunk == order[-1] else None
        acc = add_pair_sums(chunk, own, plus, minus, int_own, acc, extra, pair_dev)
    summed = acc + lax.ppermute(acc, "blk", inner_perm(1))
    summed = summed + lax.ppermute(summed, "rep", [(0, 1), (1, 0)])
    for flip in (2, 4, 8):
        summed = summed + lax.ppermute(summed, "blk", [(i, i ^ flip) for i in range(PLANES * INNER)])

    pair_irrep = jnp.bitwise_xor(
        table_lookup(pair_index[:, 0], occ_irrep), table_lookup(pair_index[:, 1], occ_irrep)
    )
    pair_energy = table_lookup(pair_index[:, 0], eps_occ) + table_lookup(pair_index[:, 1], eps_occ)
    mask = (pair_irrep[:, None] == pair_irrep[None, :]).astype(jnp.float32)
    mask = jnp.pad(mask, ((0, 0), (0, LANES - pair_total)))
    own_energy = lax.dynamic_slice_in_dim(pair_energy, blk_id * pair_dev, pair_dev)
    row_energy = lax.dynamic_slice_in_dim(eps_virt, rep_id * virt_rows, virt_rows)[:, None]
    col_energy = eps_virt[None, :]

    narrow_terms = ladder_terms(tuple(range(WIDE, CHUNKS)), own, plus, minus, summed, mask, pair_dev)
    wide_terms = ladder_terms(tuple(range(WIDE)), own, plus, minus, summed, mask, pair_dev)
    outside, inside, every = {}, {}, {}
    for flip in (2, 3, 1, 0):
        outside[flip] = lax.ppermute(narrow_terms[INNER + flip], "blk", outward_perm(flip))
    for flip in (2, 3, 1, 0):
        every[flip], inside[flip] = wide_terms[flip], narrow_terms[flip]
        if flip:
            inside[flip] = lax.ppermute(inside[flip], "blk", inner_perm(flip, (1, 2)))
            every[flip] = lax.ppermute(every[flip], "blk", inner_perm(flip))
    update = fock_term
    for flip in range(INNER):
        base = jnp.reshape((me ^ flip) * CHUNKS, (1,)).astype(jnp.int32)
        update = add_and_scale(update, [every[flip]], base, own_energy, row_energy, col_energy)
        update = add_and_scale(
            update, [inside[flip], outside[flip]], base + WIDE, own_energy, row_energy, col_energy
        )
    return update


def solution(mesh):
    fits = mesh.shape["blk"] == PLANES * INNER and mesh.shape["rep"] == 2
    return jax.shard_map(
        line_plan if fits else spread_plan,
        mesh=mesh,
        in_specs=(
            P("blk", "rep", None),
            P("blk", "rep", None),
            P("blk", None),
            P("blk", None),
            P(),
            P(),
            P(),
            P(),
            P(),
        ),
        out_specs=P("blk", "rep", None),
        check_vma=False,
    )
```

```python
import functools

import jax
import jax.numpy as jnp
from jax import lax
from jax.experimental import pallas as pl
from jax.experimental.pallas import tpu as pltpu
from jax.sharding import PartitionSpec as P

PLANES = 4
INNER = 4
CHUNK = 16
CHUNKS = 8
WIDE = 5
LANES = 128
VMEM_BYTES = 63 * 1024 * 1024


def table_lookup(index_col, table):
    iota_rows = jnp.arange(table.shape[0], dtype=jnp.int32)
    equal = index_col[:, None] == iota_rows[None, :]
    return jnp.sum(jnp.where(equal, table[None, :], jnp.zeros_like(table)[None, :]), axis=1)


def spread_plan(
    amplitudes,
    integrals,
    fock_matrix,
    hole_ladder,
    virt_irrep,
    occ_irrep,
    pair_index,
    eps_occ,
    eps_virt,
):
    pair_dev = amplitudes.shape[0]
    virt_rows = amplitudes.shape[1]
    virt_all = amplitudes.shape[2]
    blk_count = lax.axis_size("blk")
    rows_each = virt_rows // blk_count
    pair_total = pair_dev * blk_count
    blk_id = lax.axis_index("blk")
    rep_id = lax.axis_index("rep")
    piece = lax.all_gather(fock_matrix, "blk", axis=0, tiled=True)
    kept = jnp.where(virt_irrep[:, None] == virt_irrep[None, :], piece, jnp.zeros_like(piece))
    fock_term = jnp.einsum(
        "pac,bc->pab", amplitudes, kept, preferred_element_type=jnp.float32
    ).astype(jnp.bfloat16)
    amp_virt, int_virt = (
        lax.all_to_all(amplitudes, "blk", split_axis=1, concat_axis=0, tiled=True),
        lax.all_to_all(integrals, "blk", split_axis=1, concat_axis=0, tiled=True),
    )
    amp_flat = amp_virt.reshape(pair_total, rows_each * virt_all)
    int_flat = int_virt.reshape(pair_total, rows_each * virt_all)
    partial_sums = jnp.dot(amp_flat, int_flat.T, preferred_element_type=jnp.float32)
    pair_irrep = jnp.bitwise_xor(
        table_lookup(pair_index[:, 0], occ_irrep), table_lookup(pair_index[:, 1], occ_irrep)
    )
    pair_energy = table_lookup(pair_index[:, 0], eps_occ) + table_lookup(pair_index[:, 1], eps_occ)
    summed = lax.psum(partial_sums, ("rep", "blk"))
    hole_all = lax.all_gather(hole_ladder, "blk", axis=0, tiled=True)
    same_pair = pair_irrep[:, None] == pair_irrep[None, :]
    ladder = jnp.where(same_pair, hole_all + summed, jnp.zeros_like(summed)).astype(jnp.bfloat16)
    ladder_virt = jnp.dot(ladder, amp_flat, preferred_element_type=jnp.float32)
    ladder_virt = ladder_virt.reshape(pair_total, rows_each, virt_all).astype(jnp.bfloat16)
    ladder_term = lax.all_to_all(ladder_virt, "blk", split_axis=0, concat_axis=1, tiled=True)
    row_energy = lax.dynamic_slice_in_dim(eps_virt, rep_id * virt_rows, virt_rows)
    own_energy = lax.dynamic_slice_in_dim(pair_energy, blk_id * pair_dev, pair_dev)
    denom = own_energy[:, None, None] - row_energy[None, :, None] - eps_virt[None, None, :]
    total = fock_term.astype(jnp.float32) + ladder_term.astype(jnp.float32)
    return (total / denom).astype(jnp.bfloat16)


def plane_perm(step, first, last):
    return [
        (plane * INNER + at, (plane + step) * INNER + at)
        for plane in range(first, last + 1)
        for at in range(INNER)
    ]


def inner_perm(flip, planes=range(PLANES)):
    return [(p * INNER + at, p * INNER + (at ^ flip)) for p in planes for at in range(INNER)]


def outward_perm(flip):
    return [
        (p * INNER + at, q * INNER + (at ^ flip)) for p, q in ((1, 0), (2, 3)) for at in range(INNER)
    ]


def sixth(index):
    return sum((index >= edge).astype(jnp.int32) for edge in (6, 12, 18))


def pair_at(index, me, pair_dev):
    group = sixth(index)
    return pair_dev * (me ^ group) + index - pair_dev * group


def place_sources(own, plus, minus, chunk):
    table = {
        1: {0: plus.get(chunk), 1: own, 2: minus.get(chunk), 3: minus.get(CHUNKS + chunk)},
        2: {0: plus.get(CHUNKS + chunk), 1: plus.get(chunk), 2: own, 3: minus.get(chunk)},
    }
    if chunk < WIDE:
        table[0] = {0: own, 1: minus.get(chunk), 2: minus.get(WIDE + chunk), 3: minus.get(2 * WIDE + chunk)}
        table[3] = {0: plus.get(2 * WIDE + chunk), 1: plus.get(WIDE + chunk), 2: plus.get(chunk), 3: own}
    return table


def late_plane(plane):
    return PLANES - 1 if plane < 2 else 0


def numbered(arrays, chosen):
    numbers = []
    for array in chosen:
        found = [n for n, other in enumerate(arrays) if other is array]
        if not found:
            found = [len(arrays)]
            arrays.append(array)
        numbers.append(found[0])
    return numbers


def here():
    blk = lax.axis_index("blk")
    return lax.div(blk, INNER), lax.rem(blk, INNER)


def kept_sum(gram, depth):
    row_id = lax.broadcasted_iota(jnp.int32, gram.shape, 0)
    col_id = lax.broadcasted_iota(jnp.int32, gram.shape, 1)
    same = (row_id & (depth - 1)) == (col_id & (depth - 1))
    return jnp.where(same, gram, 0.0).reshape(-1, depth, gram.shape[1]).sum(axis=1)


def exact_dot(left, right):
    return jnp.dot(left, right, preferred_element_type=jnp.float32, precision=lax.Precision.HIGHEST)


def pad_rows(array):
    extra = LANES - array.shape[0]
    return jnp.concatenate([array, jnp.zeros((extra, array.shape[1]), array.dtype)], axis=0)


def pair_kernel(table, near_too, own_too, parts, late, last, pair_dev, *refs):
    acc_in, out_ref, amp, ints, turned, total, sems = refs[-7:]
    plane, me = here()
    chunks, _, rows, depth, width = amp.shape
    sides = ints.shape[1]
    total[...] = acc_in[...]
    for z, (amp_from, int_from) in table.items():

        @pl.when(plane == z)
        def _():
            for c in range(chunks):
                for n in range(sides):
                    pltpu.make_async_copy(refs[int_from[c][n]], ints.at[c, n], sems.at[c, len(parts) + n]).start()
                for n in range(len(parts)):
                    pltpu.make_async_copy(refs[amp_from[c][n]], amp.at[c, n], sems.at[c, n]).start()

    def add_all():
        for c in range(chunks):
            for n in range(sides):
                pltpu.make_async_copy(refs[0], ints.at[c, n], sems.at[c, len(parts) + n]).wait()
                turned[c, n] = ints[c, n].reshape(rows * depth, width).T
            for n in range(len(parts)):
                pltpu.make_async_copy(refs[0], amp.at[c, n], sems.at[c, n]).wait()

        def add_part(n, carry):
            if late:
                p = jnp.where(plane < 2, PLANES - 1, 0)
            else:
                p = jnp.where(plane < 2, n + parts[0], n + parts[0] + 1)
            place = pl.ds(pl.multiple_of(p * rows, 8), rows)
            for side in range(sides):
                gram = jnp.zeros((rows * depth, rows * depth), jnp.float32)
                for c in range(chunks):
                    left = amp[c, n].reshape(rows * depth, width)
                    gram += jnp.dot(left, turned[c, side], preferred_element_type=jnp.float32)
                total[side + (0 if own_too else 1), place] += kept_sum(gram, depth)
            return carry

        lax.fori_loop(0, len(parts), add_part, 0)

    if len(table) == PLANES:
        add_all()
    else:
        pl.when((plane == 1) | (plane == 2))(add_all)
    if not last:
        out_ref[...] = total[...]
        return
    hole_ref = refs[-8]
    lanes = total.shape[2]
    summed = jnp.zeros((total.shape[1], LANES), jnp.float32)
    near = jnp.where(plane < 2, 0, PLANES - 1)
    row_id = lax.broadcasted_iota(jnp.int32, (lanes, LANES), 0) // CHUNK
    col_id = lax.broadcasted_iota(jnp.int32, (lanes, LANES), 1)
    pair_id = pair_at(row_id, me, pair_dev)
    for side, at in ((0, plane), (1, near)):
        chosen = (col_id == pair_id + at * rows).astype(jnp.float32)
        summed += exact_dot(total[side], chosen)
    out_id = lax.broadcasted_iota(jnp.int32, (total.shape[1], LANES), 0)
    in_id = lax.broadcasted_iota(jnp.int32, (total.shape[1], LANES), 1)
    in_plane = sum((in_id >= p * rows).astype(jnp.int32) for p in range(1, PLANES))
    in_pair = pair_at(in_id - in_plane * rows, me, pair_dev) + in_plane * rows
    chosen = (out_id == in_pair).astype(jnp.float32)
    out_ref[...] = hole_ref[...] + exact_dot(chosen, pad_rows(summed))


def add_pair_sums(chunks, parts, own_too, near_too, own, got, int_own, acc, hole=None, after=()):
    late, last = parts is None, hole is not None
    parts = (0,) if late else parts
    rows, depth, width = own[chunks[0]].shape
    arrays, table = [], {}
    for chunk in chunks:
        for z, sources in place_sources(own[chunk], got[0], got[1], chunk).items():
            early = [sources[p] for p in range(PLANES) if p != late_plane(z)]
            amp_from = [sources[late_plane(z)]] if late else [early[n] for n in parts]
            int_from = [int_own[chunk]] if own_too else []
            if near_too:
                int_from.append(got[z - 1][CHUNKS + chunk - WIDE])
            entry = table.setdefault(z, ([], []))
            entry[0].append(numbered(arrays, amp_from))
            entry[1].append(numbered(arrays, int_from))
    sides = own_too + near_too
    operands = arrays + list(after)
    far = len(operands)
    if last:
        operands.append(hole)
    operands.append(acc)
    shape = (PLANES * rows, LANES) if last else acc.shape
    block = rows * depth
    return pl.pallas_call(
        functools.partial(pair_kernel, table, near_too, own_too, parts, late, last, rows // INNER),
        out_shape=jax.ShapeDtypeStruct(shape, jnp.float32),
        in_specs=[pl.BlockSpec(memory_space=pl.ANY)] * far
        + [pl.BlockSpec(memory_space=pltpu.VMEM)] * (len(operands) - far),
        out_specs=pl.BlockSpec(memory_space=pltpu.VMEM),
        scratch_shapes=[
            pltpu.VMEM((len(chunks), len(parts), rows, depth, width), jnp.bfloat16),
            pltpu.VMEM((len(chunks), sides, rows, depth, width), jnp.bfloat16),
            pltpu.VMEM((len(chunks), sides, width, block), jnp.bfloat16),
            pltpu.VMEM(acc.shape, jnp.float32),
            pltpu.SemaphoreType.DMA((len(chunks), len(parts) + sides)),
        ],
        compiler_params=pltpu.CompilerParams(vmem_limit_bytes=VMEM_BYTES),
        cost_estimate=pl.CostEstimate(
            flops=2 * len(chunks) * len(parts) * sides * block**2 * width,
            bytes_accessed=len(chunks) * (len(parts) + sides) * block * width * 2,
            transcendentals=0,
        ),
        name=f"pair_sums_{chunks[0]}_{'late' if late else parts[0]}",
    )(*operands)


def places_kernel(pair_dev, col_ref, row_ref, keep_ref):
    plane, me = here()
    rows, depth = INNER * pair_dev, CHUNK
    block = rows * depth
    col = lax.broadcasted_iota(jnp.int32, (LANES, PLANES * block), 1) // depth
    col_plane = sum((col >= p * rows).astype(jnp.int32) for p in range(1, PLANES))
    col_pair = pair_at(col - col_plane * rows, me, pair_dev) + col_plane * rows
    col_ref[...] = (lax.broadcasted_iota(jnp.int32, col.shape, 0) == col_pair).astype(jnp.bfloat16)
    row = lax.broadcasted_iota(jnp.int32, (block, LANES), 0) // depth
    row_pair = pair_at(row, me, pair_dev)
    for side, at in enumerate((plane, jnp.where(plane < 2, 0, PLANES - 1))):
        chosen = lax.broadcasted_iota(jnp.int32, row.shape, 1) == row_pair + at * rows
        row_ref[side] = chosen.astype(jnp.bfloat16)
    left = lax.broadcasted_iota(jnp.int32, (block, PLANES * block), 0) & (depth - 1)
    right = lax.broadcasted_iota(jnp.int32, (block, PLANES * block), 1) & (depth - 1)
    keep_ref[...] = (left == right).astype(jnp.bfloat16)


def ladder_places(pair_dev):
    block = INNER * pair_dev * CHUNK
    shapes = [(LANES, PLANES * block), (2, block, LANES), (block, PLANES * block)]
    return pl.pallas_call(
        functools.partial(places_kernel, pair_dev),
        out_shape=[jax.ShapeDtypeStruct(shape, jnp.bfloat16) for shape in shapes],
        out_specs=[pl.BlockSpec(memory_space=pltpu.VMEM)] * 3,
        compiler_params=pltpu.CompilerParams(vmem_limit_bytes=VMEM_BYTES),
        name="ladder_places",
    )()


def ladder_kernel(table_of, wide, pair_dev, *refs):
    sides = 1 if wide else 2
    own = refs[0]
    count = sides * INNER
    sum_ref, mask_ref, col_ref, row_ref, keep_ref = refs[-8 - count : -3 - count]
    outs = refs[-3 - count : -3]
    amp, spread, sems = refs[-3:]
    plane, _ = here()
    rows, depth, width = amp.shape[2:]
    block = rows * depth
    for z, table in table_of.items():

        @pl.when(plane == z)
        def _():
            for n, sources in enumerate(table):
                for p in range(PLANES):
                    pltpu.make_async_copy(refs[sources[p]], amp.at[n, p], sems.at[n, p]).start()

    def work():
        ladder = jnp.where(mask_ref[...] > 0, sum_ref[...], 0.0).astype(jnp.bfloat16)
        ladder = pad_rows(ladder)
        for side in range(sides):
            picked = jnp.dot(row_ref[side], ladder, preferred_element_type=jnp.float32).astype(jnp.bfloat16)
            full = jnp.dot(picked, col_ref[...], preferred_element_type=jnp.float32).astype(jnp.bfloat16)
            spread[side] = jnp.where(keep_ref[...] > 0, full, jnp.zeros_like(full))

        def one_chunk(n, carry):
            for p in range(PLANES):
                pltpu.make_async_copy(own, amp.at[n, p], sems.at[n, p]).wait()
            columns = amp[n].reshape(PLANES * block, width)
            place = pl.ds(pl.multiple_of(n * depth, depth), depth)
            for side in range(sides):
                term = jnp.dot(spread[side], columns, preferred_element_type=jnp.float32).astype(jnp.bfloat16)
                term = term.reshape(INNER, pair_dev, depth, width)
                for flip in range(INNER):
                    outs[side * INNER + flip][:, place, :] = term[flip]
            return carry

        lax.fori_loop(0, amp.shape[0], one_chunk, 0)

    if wide:
        work()
    else:
        pl.when((plane == 1) | (plane == 2))(work)


def ladder_terms(chunks, own, plus, minus, summed, mask, places, after=()):
    rows, depth, width = own[chunks[0]].shape
    pair_dev = rows // INNER
    wide = chunks[0] < WIDE
    arrays, table = [], {}
    for chunk in chunks:
        for z, sources in place_sources(own[chunk], plus, minus, chunk).items():
            table.setdefault(z, []).append(numbered(arrays, [sources[p] for p in range(PLANES)]))
    operands = arrays + list(after)
    far = len(operands)
    operands += [summed, mask, *places]
    sides = 1 if wide else 2
    block = rows * depth
    return pl.pallas_call(
        functools.partial(ladder_kernel, table, wide, pair_dev),
        out_shape=[jax.ShapeDtypeStruct((pair_dev, len(chunks) * depth, width), jnp.bfloat16)] * (sides * INNER),
        in_specs=[pl.BlockSpec(memory_space=pl.ANY)] * far
        + [pl.BlockSpec(memory_space=pltpu.VMEM)] * (len(operands) - far),
        out_specs=[pl.BlockSpec(memory_space=pltpu.VMEM)] * (sides * INNER),
        scratch_shapes=[
            pltpu.VMEM((len(chunks), PLANES, rows, depth, width), jnp.bfloat16),
            pltpu.VMEM((sides, block, PLANES * block), jnp.bfloat16),
            pltpu.SemaphoreType.DMA((len(chunks), PLANES)),
        ],
        compiler_params=pltpu.CompilerParams(vmem_limit_bytes=VMEM_BYTES),
        cost_estimate=pl.CostEstimate(
            flops=2 * PLANES * block * block * width * sides * len(chunks),
            bytes_accessed=(PLANES + sides) * block * width * 2 * len(chunks),
            transcendentals=0,
        ),
        name=f"ladder_{chunks[0]}",
    )(*operands)


def scale_kernel(flip, first, count, fock_ref, inverse_ref, *refs):
    pieces, (out_ref, fock, inverse, ladder, sems) = refs[:count], refs[count:]
    plane, me = here()
    pair_dev, rows, _ = fock.shape
    start = pl.multiple_of((me ^ flip) * (CHUNK * CHUNKS) + first * CHUNK, CHUNK)
    place = pl.ds(start, rows)

    def load(p):
        return (
            pltpu.make_async_copy(fock_ref.at[p, place], fock.at[p], sems.at[p, 0]),
            pltpu.make_async_copy(inverse_ref.at[p, place], inverse.at[p], sems.at[p, 1]),
        )

    def piece(p, source):
        return pltpu.make_async_copy(source.at[p], ladder.at[p], sems.at[p, 2])

    def store(p):
        return pltpu.make_async_copy(fock.at[p], out_ref.at[p, place], sems.at[p, 3])

    middle = (plane == 1) | (plane == 2)
    for p in range(pair_dev):
        for copy in load(p):
            copy.start()
        if count == 1:
            piece(p, pieces[0]).start()
        else:
            pl.when(middle)(piece(p, pieces[0]).start)
            pl.when(jnp.logical_not(middle))(piece(p, pieces[1]).start)

    def one_pair(p, carry):
        for copy in (*load(p), piece(p, pieces[0])):
            copy.wait()
        total = fock[p].astype(jnp.float32) + ladder[p].astype(jnp.float32)
        fock[p] = (total * inverse[p]).astype(fock.dtype)
        store(p).start()
        return carry

    lax.fori_loop(0, pair_dev, one_pair, 0)
    for p in range(pair_dev):
        store(p).wait()


def add_and_scale(buffer, inverse, pieces, flip, first):
    shape = pieces[0].shape
    size = shape[0] * shape[1] * shape[2]
    return pl.pallas_call(
        functools.partial(scale_kernel, flip, first, len(pieces)),
        out_shape=jax.ShapeDtypeStruct(buffer.shape, buffer.dtype),
        in_specs=[pl.BlockSpec(memory_space=pl.ANY)] * (2 + len(pieces)),
        out_specs=pl.BlockSpec(memory_space=pl.ANY),
        scratch_shapes=[
            pltpu.VMEM(shape, buffer.dtype),
            pltpu.VMEM(shape, jnp.float32),
            pltpu.VMEM(shape, buffer.dtype),
            pltpu.SemaphoreType.DMA((shape[0], 4)),
        ],
        input_output_aliases={0: 0},
        compiler_params=pltpu.CompilerParams(vmem_limit_bytes=VMEM_BYTES),
        cost_estimate=pl.CostEstimate(
            flops=2 * size, bytes_accessed=(8 + 2 * len(pieces)) * size, transcendentals=0
        ),
        name="add_and_scale",
    )(buffer, inverse, *pieces)


def move_kernel(moves, count, *refs):
    outs, sems = refs[count:-1], refs[-1]
    _, me = here()
    copies = []
    for n, (source, flip, at, target, place) in enumerate(moves):
        ref = refs[source]
        if flip is None:
            ref = ref.at[at]
        else:
            start = pl.multiple_of((me ^ flip) * (CHUNK * CHUNKS) + at.start, CHUNK)
            ref = ref.at[:, pl.ds(start, at.stop - at.start), :]
        copies.append(pltpu.make_async_copy(ref, outs[target].at[place], sems.at[n]))
    for copy in copies:
        copy.start()
    for copy in copies:
        copy.wait()


def move(operands, shapes, moves, name):
    moved = 2 * sum(2 * shape[0] * shape[-2] * shape[-1] for shape in shapes)
    call = pl.pallas_call(
        functools.partial(move_kernel, moves, len(operands)),
        out_shape=[jax.ShapeDtypeStruct(shape, jnp.bfloat16) for shape in shapes],
        in_specs=[pl.BlockSpec(memory_space=pl.ANY)] * len(operands),
        out_specs=[pl.BlockSpec(memory_space=pltpu.VMEM)] * len(shapes),
        scratch_shapes=[pltpu.SemaphoreType.DMA((len(moves),))],
        compiler_params=pltpu.CompilerParams(vmem_limit_bytes=VMEM_BYTES),
        cost_estimate=pl.CostEstimate(flops=0, bytes_accessed=moved, transcendentals=0),
        name=name,
    )
    return list(call(*operands))


def rows_of(chunk, first=0):
    return slice((chunk - first) * CHUNK, (chunk - first + 1) * CHUNK)


def core_moves(source, group, target):
    rows = slice(group[0] * CHUNK, group[1] * CHUNK)
    return [(source, 1 + 2 * side, rows, target, (slice(None), side)) for side in range(2)]


def across_moves(source, core, first, group, pair_dev, target):
    rows = slice(group[0] * CHUNK, group[1] * CHUNK)
    near = slice((group[0] - first) * CHUNK, (group[1] - first) * CHUNK)
    return [
        (source, 2, rows, target, slice(0, pair_dev)),
        (core, None, (slice(None), 1, near), target, slice(pair_dev, 2 * pair_dev)),
    ]


def own_moves(source, core, first, across, group, pair_dev, target):
    moves = []
    for n, chunk in enumerate(range(*group)):
        moves += [
            (source, 0, rows_of(chunk), target + n, slice(0, pair_dev)),
            (core, None, (slice(None), 0, rows_of(chunk, first)), target + n, slice(pair_dev, 2 * pair_dev)),
            (across, None, (slice(None), rows_of(chunk, group[0])), target + n, slice(2 * pair_dev, 4 * pair_dev)),
        ]
    return moves


def pick_kernel(choices, *refs):
    outs, sems = refs[-3:-1], refs[-1]
    plane, _ = here()

    def each(do):
        for n, table in enumerate(choices):
            for far, source in table.items():
                at = far if n == 0 else PLANES - 1 - far
                copy = pltpu.make_async_copy(refs[source], outs[n], sems.at[n])
                pl.when(plane == at)(getattr(copy, do))

    each("start")
    each("wait")


def pick(choices, name, after=()):
    arrays = []
    tables = [dict(zip(table, numbered(arrays, table.values()))) for table in choices]
    example = arrays[0]
    arrays += after
    size = example.size
    return pl.pallas_call(
        functools.partial(pick_kernel, tables),
        out_shape=[jax.ShapeDtypeStruct(example.shape, example.dtype)] * 2,
        in_specs=[pl.BlockSpec(memory_space=pl.ANY)] * len(arrays),
        out_specs=[pl.BlockSpec(memory_space=pltpu.VMEM)] * 2,
        scratch_shapes=[pltpu.SemaphoreType.DMA((2,))],
        compiler_params=pltpu.CompilerParams(vmem_limit_bytes=VMEM_BYTES),
        cost_estimate=pl.CostEstimate(flops=0, bytes_accessed=8 * size, transcendentals=0),
        name=name,
    )(*arrays)


def line_round(step, own, int_own, got, after, done_with):
    narrow = CHUNKS - WIDE
    first, last = 0, 2
    choices = []
    for have in got:
        if step < WIDE:
            table = {far: own[step] for far in range(3)}
        elif step < CHUNKS:
            table = {0: own[step], 1: own[step], 2: have[step - WIDE]}
        else:
            table = {1: have[step - CHUNKS]}
            if step < CHUNKS + narrow:
                table[0] = int_own[WIDE + step - CHUNKS]
            else:
                first = 1
            if step < 2 * WIDE:
                table[2] = have[step - WIDE]
            elif step < 3 * WIDE:
                table[2] = have[step - 2 * WIDE + CHUNKS]
            else:
                last = 1
        choices.append(table)
    if not after and (step < WIDE or first == last):
        sends = [table[1] for table in choices]
    else:
        sends = done_with(list(pick(choices, f"pick_{step}", after)))
    got[0][step] = lax.ppermute(sends[0], "blk", plane_perm(1, first, last))
    got[1][step] = lax.ppermute(sends[1], "blk", plane_perm(-1, PLANES - 1 - last, PLANES - 1 - first))


def line_exchanges(amplitudes, integrals, hole, beside, beside_later):
    pair_dev, _, width = amplitudes.shape
    rows = INNER * pair_dev
    full = (rows, CHUNK, width)
    own, int_own, got = {}, {}, ({}, {})

    def across_shape(group):
        return (2 * pair_dev, (group[1] - group[0]) * CHUNK, width)

    last = []

    def in_turn(operands):
        return list(operands) + last

    def done_with(found):
        last[:] = found[:1]
        return found

    def arrived(step):
        return [have[step] for have in got]

    def rounds(*steps, after=()):
        for step in steps:
            before = arrived(step - 2) if step >= 2 else []
            line_round(step, own, int_own, got, in_turn(before + list(after)) if step >= 2 else [], done_with)

    groups = ((0, 1), (1, 2), (2, 4), (4, 6), (6, CHUNKS))
    core_groups = ((0, 2), (2, CHUNKS))
    cores = move(
        [amplitudes],
        [(pair_dev, 2, (end - first) * CHUNK, width) for first, end in core_groups],
        [one for n, group in enumerate(core_groups) for one in core_moves(0, group, n)],
        "move_core",
    )
    cores = [lax.ppermute(core, "blk", inner_perm(1)) for core in cores]
    (across,) = move(
        [amplitudes, cores[0]],
        [across_shape(groups[0])],
        across_moves(0, 1, 0, groups[0], pair_dev, 0),
        "move_across",
    )
    waits = ((), (), (0,), (2,), (4,))
    int_groups = ((WIDE, CHUNKS), (0, WIDE))
    for n, group in enumerate(groups):
        across = lax.ppermute(across, "blk", inner_perm(2))
        size = group[1] - group[0]
        mine = int(group[0] >= core_groups[1][0])
        moves = own_moves(0, 1, core_groups[mine][0], 2, group, pair_dev, 0)
        shapes = [full] * size
        operands = [amplitudes, cores[mine], across]
        if n + 1 < len(groups):
            then = int(groups[n + 1][0] >= core_groups[1][0])
            moves += across_moves(0, 3, core_groups[then][0], groups[n + 1], pair_dev, size)
            shapes.append(across_shape(groups[n + 1]))
            operands.append(cores[then])
        else:
            moves += across_moves(3, 4, 0, int_groups[0], pair_dev, size)
            shapes.append(across_shape(int_groups[0]))
            operands += [integrals, int_core]
        if n == 3:
            moves += core_moves(4, (0, CHUNKS), size + 1)
            shapes.append((pair_dev, 2, CHUNKS * CHUNK, width))
            operands.append(integrals)
        if n == 2:
            operands += beside
        for step in waits[n]:
            operands += arrived(step)
        found = done_with(move(in_turn(operands), shapes, moves, f"move_own_{group[0]}"))
        own.update(zip(range(*group), found))
        across = found[size]
        if n == 3:
            int_core = lax.ppermute(found[size + 1], "blk", inner_perm(1))
        rounds(*((0,), (1,), (2, 3), (4, 5), (6,))[n])
    rounds(7, after=beside_later[1:])

    def own_integrals(n, across):
        group = int_groups[n]
        across = lax.ppermute(across, "blk", inner_perm(2))
        size = group[1] - group[0]
        moves = own_moves(0, 1, 0, 2, group, pair_dev, 0)
        shapes = [full] * size
        if n + 1 < len(int_groups):
            moves += across_moves(0, 1, 0, int_groups[n + 1], pair_dev, size)
            shapes.append(across_shape(int_groups[n + 1]))
        found = done_with(move(in_turn([integrals, int_core, across]), shapes, moves, f"move_ints_{group[0]}"))
        int_own.update(zip(range(*group), found))
        return found[-1]

    wide, narrow = tuple(range(WIDE)), tuple(range(WIDE, CHUNKS))
    acc = jnp.zeros((2, PLANES * rows, rows * CHUNK), jnp.float32)

    def add(*what, acc, **more):
        return done_with([add_pair_sums(*what, own, got, int_own, acc, after=in_turn([]), **more)])[0]

    across = own_integrals(0, across)
    rounds(8)
    acc = add(narrow, (0, 1, 2), True, False, acc=acc)
    rounds(9)
    rounds(10, after=beside_later[:1])
    rounds(11)
    own_integrals(1, across)
    for part in range(3):
        acc = add(wide, (part,), True, False, acc=acc)
        rounds(12 + part)
    acc = add(narrow, (0, 1, 2), False, True, acc=acc)
    rounds(15)
    acc = add(wide[:3], None, True, False, acc=acc)
    acc = add(wide[3:], None, True, False, acc=acc)
    acc = add(narrow[:-1], None, True, True, acc=acc)
    acc = add(narrow[-1:], None, True, True, acc=acc, hole=hole)
    return own, *got, acc


def line_plan(
    amplitudes,
    integrals,
    fock_matrix,
    hole_ladder,
    virt_irrep,
    occ_irrep,
    pair_index,
    eps_occ,
    eps_virt,
):
    pair_dev, virt_rows, virt_all = amplitudes.shape
    pair_total = pair_dev * PLANES * INNER
    blk_id = lax.axis_index("blk")
    rep_id = lax.axis_index("rep")
    plane, me = here()
    half = virt_all // 2
    piece = lax.dynamic_slice_in_dim(fock_matrix, rep_id * half, half, axis=1)
    piece = lax.all_gather(piece, "blk", axis=0, tiled=True)
    fock_all = lax.all_gather(piece, "rep", axis=1, tiled=True)
    kept = jnp.where(virt_irrep[:, None] == virt_irrep[None, :], fock_all, jnp.zeros_like(fock_all))
    fock_term = jnp.einsum(
        "pac,bc->pab", amplitudes, kept, preferred_element_type=jnp.float32
    ).astype(jnp.bfloat16)

    pair_irrep = jnp.bitwise_xor(
        table_lookup(pair_index[:, 0], occ_irrep), table_lookup(pair_index[:, 1], occ_irrep)
    )
    pair_energy = table_lookup(pair_index[:, 0], eps_occ) + table_lookup(pair_index[:, 1], eps_occ)
    mask = (pair_irrep[:, None] == pair_irrep[None, :]).astype(jnp.float32)
    mask = jnp.pad(mask, ((0, 0), (0, LANES - pair_total)))
    own_energy = lax.dynamic_slice_in_dim(pair_energy, blk_id * pair_dev, pair_dev)
    row_energy = lax.dynamic_slice_in_dim(eps_virt, rep_id * virt_rows, virt_rows)
    inverse = 1.0 / (own_energy[:, None, None] - row_energy[None, :, None] - eps_virt[None, None, :])

    hole = jnp.zeros((pair_total, LANES), jnp.float32)
    hole_rows = jnp.pad(hole_ladder, ((0, 0), (0, LANES - pair_total)))
    hole = lax.dynamic_update_slice_in_dim(hole, hole_rows, blk_id * pair_dev, axis=0)
    hole = jnp.where(rep_id == 0, hole, jnp.zeros_like(hole))
    places = ladder_places(pair_dev)
    own, plus, minus, acc = line_exchanges(
        amplitudes, integrals, hole, [piece], [fock_term, inverse, mask, places[2]]
    )
    summed = acc + lax.ppermute(acc, "blk", inner_perm(1))
    summed = summed + lax.ppermute(summed, "rep", [(0, 1), (1, 0)])
    for flip in (2, 4, 8):
        summed = summed + lax.ppermute(summed, "blk", [(i, i ^ flip) for i in range(PLANES * INNER)])

    terms = functools.partial(ladder_terms, own=own, plus=plus, minus=minus, summed=summed, mask=mask, places=places)
    ladder_groups = (tuple(range(WIDE, CHUNKS)), tuple(range(2)), tuple(range(2, WIDE)))
    outside, inside = {}, {}
    narrow = terms(ladder_groups[0])
    for flip in (2, 3):
        inside[0, flip] = lax.ppermute(narrow[flip], "blk", inner_perm(flip, (1, 2)))
        outside[flip] = lax.ppermute(narrow[INNER + flip], "blk", outward_perm(flip))
    for flip in (0, 1):
        outside[flip] = lax.ppermute(narrow[INNER + flip], "blk", outward_perm(flip))
    inside[0, 1] = lax.ppermute(narrow[1], "blk", inner_perm(1, (1, 2)))
    inside[0, 0] = narrow[0]
    for n in (1, 2):
        wide = terms(ladder_groups[n], after=[inside[0, 2], outside[2]] if n == 2 else [narrow[0]])
        inside[n, 0] = wide[0]
        for flip in (2, 3, 1):
            inside[n, flip] = lax.ppermute(wide[flip], "blk", inner_perm(flip))
    update = fock_term
    order = ((1, 0), (1, 1), (2, 0), (2, 1), (0, 2), (0, 3), (0, 1), (0, 0), (1, 2), (1, 3), (2, 2), (2, 3))
    for n, flip in order:
        pieces = [inside[n, flip]] + ([outside[flip]] if n == 0 else [])
        update = add_and_scale(update, inverse, pieces, flip, ladder_groups[n][0])
    return update


def solution(mesh):
    fits = mesh.shape["blk"] == PLANES * INNER and mesh.shape["rep"] == 2
    return jax.shard_map(
        line_plan if fits else spread_plan,
        mesh=mesh,
        in_specs=(
            P("blk", "rep", None),
            P("blk", "rep", None),
            P("blk", None),
            P("blk", None),
            P(),
            P(),
            P(),
            P(),
            P(),
        ),
        out_specs=P("blk", "rep", None),
        check_vma=False,
    )
```

```python
import functools

import jax
import jax.numpy as jnp
from jax import lax
from jax.experimental import pallas as pl
from jax.experimental.pallas import tpu as pltpu
from jax.sharding import PartitionSpec as P

PLANES = 4
INNER = 4
CHUNK = 16
HALF = 8
CHUNKS = 8
WIDE = 5
LANES = 128
VMEM_BYTES = 63 * 1024 * 1024


def table_lookup(index_col, table):
    iota_rows = jnp.arange(table.shape[0], dtype=jnp.int32)
    equal = index_col[:, None] == iota_rows[None, :]
    return jnp.sum(jnp.where(equal, table[None, :], jnp.zeros_like(table)[None, :]), axis=1)


def spread_plan(
    amplitudes,
    integrals,
    fock_matrix,
    hole_ladder,
    virt_irrep,
    occ_irrep,
    pair_index,
    eps_occ,
    eps_virt,
):
    pair_dev = amplitudes.shape[0]
    virt_rows = amplitudes.shape[1]
    virt_all = amplitudes.shape[2]
    blk_count = lax.axis_size("blk")
    rows_each = virt_rows // blk_count
    pair_total = pair_dev * blk_count
    blk_id = lax.axis_index("blk")
    rep_id = lax.axis_index("rep")
    piece = lax.all_gather(fock_matrix, "blk", axis=0, tiled=True)
    kept = jnp.where(virt_irrep[:, None] == virt_irrep[None, :], piece, jnp.zeros_like(piece))
    fock_term = jnp.einsum(
        "pac,bc->pab", amplitudes, kept, preferred_element_type=jnp.float32
    ).astype(jnp.bfloat16)
    amp_virt, int_virt = (
        lax.all_to_all(amplitudes, "blk", split_axis=1, concat_axis=0, tiled=True),
        lax.all_to_all(integrals, "blk", split_axis=1, concat_axis=0, tiled=True),
    )
    amp_flat = amp_virt.reshape(pair_total, rows_each * virt_all)
    int_flat = int_virt.reshape(pair_total, rows_each * virt_all)
    partial_sums = jnp.dot(amp_flat, int_flat.T, preferred_element_type=jnp.float32)
    pair_irrep = jnp.bitwise_xor(
        table_lookup(pair_index[:, 0], occ_irrep), table_lookup(pair_index[:, 1], occ_irrep)
    )
    pair_energy = table_lookup(pair_index[:, 0], eps_occ) + table_lookup(pair_index[:, 1], eps_occ)
    summed = lax.psum(partial_sums, ("rep", "blk"))
    hole_all = lax.all_gather(hole_ladder, "blk", axis=0, tiled=True)
    same_pair = pair_irrep[:, None] == pair_irrep[None, :]
    ladder = jnp.where(same_pair, hole_all + summed, jnp.zeros_like(summed)).astype(jnp.bfloat16)
    ladder_virt = jnp.dot(ladder, amp_flat, preferred_element_type=jnp.float32)
    ladder_virt = ladder_virt.reshape(pair_total, rows_each, virt_all).astype(jnp.bfloat16)
    ladder_term = lax.all_to_all(ladder_virt, "blk", split_axis=0, concat_axis=1, tiled=True)
    row_energy = lax.dynamic_slice_in_dim(eps_virt, rep_id * virt_rows, virt_rows)
    own_energy = lax.dynamic_slice_in_dim(pair_energy, blk_id * pair_dev, pair_dev)
    denom = own_energy[:, None, None] - row_energy[None, :, None] - eps_virt[None, None, :]
    total = fock_term.astype(jnp.float32) + ladder_term.astype(jnp.float32)
    return (total / denom).astype(jnp.bfloat16)


def plane_perm(step, first, last):
    return [
        (plane * INNER + at, (plane + step) * INNER + at)
        for plane in range(first, last + 1)
        for at in range(INNER)
    ]


def inner_perm(flip, planes=range(PLANES)):
    return [(p * INNER + at, p * INNER + (at ^ flip)) for p in planes for at in range(INNER)]


def outward_perm(flip):
    return [
        (p * INNER + at, q * INNER + (at ^ flip)) for p, q in ((1, 0), (2, 3)) for at in range(INNER)
    ]


def sixth(index):
    return sum((index >= edge).astype(jnp.int32) for edge in (6, 12, 18))


def pair_at(index, me, pair_dev):
    group = sixth(index)
    return pair_dev * (me ^ group) + index - pair_dev * group


def place_sources(own, plus, minus, chunk):
    table = {
        1: {0: plus.get(chunk), 1: own, 2: minus.get(chunk), 3: minus.get(CHUNKS + chunk)},
        2: {0: plus.get(CHUNKS + chunk), 1: plus.get(chunk), 2: own, 3: minus.get(chunk)},
    }
    if chunk < WIDE:
        table[0] = {0: own, 1: minus.get(chunk), 2: minus.get(WIDE + chunk), 3: minus.get(2 * WIDE + chunk)}
        table[3] = {0: plus.get(2 * WIDE + chunk), 1: plus.get(WIDE + chunk), 2: plus.get(chunk), 3: own}
    return table


def late_plane(plane):
    return PLANES - 1 if plane < 2 else 0


def numbered(arrays, chosen):
    numbers = []
    for array in chosen:
        found = [n for n, other in enumerate(arrays) if other is array]
        if not found:
            found = [len(arrays)]
            arrays.append(array)
        numbers.append(found[0])
    return numbers


def here():
    blk = lax.axis_index("blk")
    return lax.div(blk, INNER), lax.rem(blk, INNER)


def kept_sum(gram, depth):
    row_id = lax.broadcasted_iota(jnp.int32, gram.shape, 0)
    col_id = lax.broadcasted_iota(jnp.int32, gram.shape, 1)
    same = (row_id & (depth - 1)) == (col_id & (depth - 1))
    return jnp.where(same, gram, 0.0).reshape(-1, depth, gram.shape[1]).sum(axis=1)


def split_rows(block):
    pairs, depth, width = block.shape
    wide = block.astype(jnp.float32).reshape(pairs, depth // HALF, HALF, width)
    return [wide[:, n].reshape(pairs * HALF, width).astype(block.dtype) for n in range(depth // HALF)]


def exact_dot(left, right):
    return jnp.dot(left, right, preferred_element_type=jnp.float32, precision=lax.Precision.HIGHEST)


def pad_rows(array):
    extra = LANES - array.shape[0]
    return jnp.concatenate([array, jnp.zeros((extra, array.shape[1]), array.dtype)], axis=0)


def pair_kernel(table, near_too, own_too, parts, late, last, pair_dev, *refs):
    acc_in, out_ref, amp, ints, turned, total, sems = refs[-7:]
    plane, me = here()
    chunks, _, rows, depth, width = amp.shape
    sides = ints.shape[1]
    total[...] = acc_in[...]
    for z, (amp_from, int_from) in table.items():

        @pl.when(plane == z)
        def _():
            for c in range(chunks):
                for n in range(sides):
                    pltpu.make_async_copy(refs[int_from[c][n]], ints.at[c, n], sems.at[c, len(parts) + n]).start()
                for n in range(len(parts)):
                    pltpu.make_async_copy(refs[amp_from[c][n]], amp.at[c, n], sems.at[c, n]).start()

    def add_all():
        for c in range(chunks):
            for n in range(sides):
                pltpu.make_async_copy(refs[0], ints.at[c, n], sems.at[c, len(parts) + n]).wait()
                for h, half in enumerate(split_rows(ints[c, n])):
                    turned[c, h, n * rows * HALF : (n + 1) * rows * HALF] = half
            for n in range(len(parts)):
                pltpu.make_async_copy(refs[0], amp.at[c, n], sems.at[c, n]).wait()

        def add_part(n, carry):
            if late:
                p = jnp.where(plane < 2, PLANES - 1, 0)
            else:
                p = jnp.where(plane < 2, n + parts[0], n + parts[0] + 1)
            place = pl.ds(pl.multiple_of(p * rows, 8), rows)
            gram = jnp.zeros((rows * HALF, sides * rows * HALF), jnp.float32)
            for c in range(chunks):
                for h, half in enumerate(split_rows(amp[c, n])):
                    gram += lax.dot_general(
                        half, turned[c, h], (((1,), (1,)), ((), ())), preferred_element_type=jnp.float32
                    )
            for side in range(sides):
                kept = kept_sum(gram[:, side * rows * HALF : (side + 1) * rows * HALF], HALF)
                total[side + (0 if own_too else 1), place] += kept
            return carry

        lax.fori_loop(0, len(parts), add_part, 0)

    if len(table) == PLANES:
        add_all()
    else:
        pl.when((plane == 1) | (plane == 2))(add_all)
    if not last:
        out_ref[...] = total[...]
        return
    hole_ref = refs[-8]
    lanes = total.shape[2]
    summed = jnp.zeros((total.shape[1], LANES), jnp.float32)
    near = jnp.where(plane < 2, 0, PLANES - 1)
    row_id = lax.broadcasted_iota(jnp.int32, (lanes, LANES), 0) // HALF
    col_id = lax.broadcasted_iota(jnp.int32, (lanes, LANES), 1)
    pair_id = pair_at(row_id, me, pair_dev)
    for side, at in ((0, plane), (1, near)):
        chosen = (col_id == pair_id + at * rows).astype(jnp.float32)
        summed += exact_dot(total[side], chosen)
    out_id = lax.broadcasted_iota(jnp.int32, (total.shape[1], LANES), 0)
    in_id = lax.broadcasted_iota(jnp.int32, (total.shape[1], LANES), 1)
    in_plane = sum((in_id >= p * rows).astype(jnp.int32) for p in range(1, PLANES))
    in_pair = pair_at(in_id - in_plane * rows, me, pair_dev) + in_plane * rows
    chosen = (out_id == in_pair).astype(jnp.float32)
    out_ref[...] = hole_ref[...] + exact_dot(chosen, pad_rows(summed))


def add_pair_sums(chunks, parts, own_too, near_too, own, got, int_own, acc, hole=None, after=()):
    late, last = parts is None, hole is not None
    parts = (0,) if late else parts
    rows, depth, width = own[chunks[0]].shape
    arrays, table = [], {}
    for chunk in chunks:
        for z, sources in place_sources(own[chunk], got[0], got[1], chunk).items():
            early = [sources[p] for p in range(PLANES) if p != late_plane(z)]
            amp_from = [sources[late_plane(z)]] if late else [early[n] for n in parts]
            int_from = [int_own[chunk]] if own_too else []
            if near_too:
                int_from.append(got[z - 1][CHUNKS + 1 + chunk - WIDE])
            entry = table.setdefault(z, ([], []))
            entry[0].append(numbered(arrays, amp_from))
            entry[1].append(numbered(arrays, int_from))
    sides = own_too + near_too
    operands = arrays + list(after)
    far = len(operands)
    if last:
        operands.append(hole)
    operands.append(acc)
    shape = (PLANES * rows, LANES) if last else acc.shape
    block = rows * depth
    return pl.pallas_call(
        functools.partial(pair_kernel, table, near_too, own_too, parts, late, last, rows // INNER),
        out_shape=jax.ShapeDtypeStruct(shape, jnp.float32),
        in_specs=[pl.BlockSpec(memory_space=pl.ANY)] * far
        + [pl.BlockSpec(memory_space=pltpu.VMEM)] * (len(operands) - far),
        out_specs=pl.BlockSpec(memory_space=pltpu.VMEM),
        scratch_shapes=[
            pltpu.VMEM((len(chunks), len(parts), rows, depth, width), jnp.bfloat16),
            pltpu.VMEM((len(chunks), sides, rows, depth, width), jnp.bfloat16),
            pltpu.VMEM((len(chunks), depth // HALF, sides * rows * HALF, width), jnp.bfloat16),
            pltpu.VMEM(acc.shape, jnp.float32),
            pltpu.SemaphoreType.DMA((len(chunks), len(parts) + sides)),
        ],
        compiler_params=pltpu.CompilerParams(vmem_limit_bytes=VMEM_BYTES),
        cost_estimate=pl.CostEstimate(
            flops=2 * len(chunks) * len(parts) * sides * block**2 * width,
            bytes_accessed=len(chunks) * (len(parts) + sides) * block * width * 2,
            transcendentals=0,
        ),
        name=f"pair_sums_{chunks[0]}_{'late' if late else parts[0]}",
    )(*operands)


def places_kernel(pair_dev, col_ref, row_ref, keep_ref):
    plane, me = here()
    rows, depth = INNER * pair_dev, HALF
    block = rows * depth
    col = lax.broadcasted_iota(jnp.int32, (LANES, PLANES * block), 1) // depth
    col_plane = sum((col >= p * rows).astype(jnp.int32) for p in range(1, PLANES))
    col_pair = pair_at(col - col_plane * rows, me, pair_dev) + col_plane * rows
    col_ref[...] = (lax.broadcasted_iota(jnp.int32, col.shape, 0) == col_pair).astype(jnp.bfloat16)
    row = lax.broadcasted_iota(jnp.int32, (block, LANES), 0) // depth
    row_pair = pair_at(row, me, pair_dev)
    for side, at in enumerate((plane, jnp.where(plane < 2, 0, PLANES - 1))):
        chosen = lax.broadcasted_iota(jnp.int32, row.shape, 1) == row_pair + at * rows
        row_ref[side] = chosen.astype(jnp.bfloat16)
    left = lax.broadcasted_iota(jnp.int32, (block, PLANES * block), 0) & (depth - 1)
    right = lax.broadcasted_iota(jnp.int32, (block, PLANES * block), 1) & (depth - 1)
    keep_ref[...] = (left == right).astype(jnp.bfloat16)


def ladder_places(pair_dev):
    block = INNER * pair_dev * HALF
    shapes = [(LANES, PLANES * block), (2, block, LANES), (block, PLANES * block)]
    return pl.pallas_call(
        functools.partial(places_kernel, pair_dev),
        out_shape=[jax.ShapeDtypeStruct(shape, jnp.bfloat16) for shape in shapes],
        out_specs=[pl.BlockSpec(memory_space=pltpu.VMEM)] * 3,
        compiler_params=pltpu.CompilerParams(vmem_limit_bytes=VMEM_BYTES),
        name="ladder_places",
    )()


def ladder_kernel(table_of, wide_count, pair_dev, *refs):
    own = refs[0]
    outs = refs[-8 - 3 * INNER : -8]
    sum_ref, mask_ref, col_ref, row_ref, keep_ref = refs[-13 - 3 * INNER : -8 - 3 * INNER]
    amp, near_spread, wide_spread, halves, near_terms, wide_terms, in_sems, out_sems = refs[-8:]
    chunks, _, rows, depth, width = amp.shape
    narrow_count = chunks - wide_count
    plane, _ = here()
    middle = (plane == 1) | (plane == 2)
    for z, table in table_of.items():

        @pl.when(plane == z)
        def _():
            for n, sources in enumerate(table):
                if sources is not None:
                    for p in range(PLANES):
                        pltpu.make_async_copy(refs[sources[p]], amp.at[n, p], in_sems.at[n, p]).start()

    ladder = jnp.where(mask_ref[...] > 0, sum_ref[...], 0.0).astype(jnp.bfloat16)
    ladder = pad_rows(ladder)

    def spread_of(side):
        picked = jnp.dot(row_ref[side], ladder, preferred_element_type=jnp.float32).astype(jnp.bfloat16)
        full = jnp.dot(picked, col_ref[...], preferred_element_type=jnp.float32).astype(jnp.bfloat16)
        return jnp.where(keep_ref[...] > 0, full, jnp.zeros_like(full))

    size = rows * HALF
    wide_spread[...] = spread_of(0)

    def store(terms, first_out, n, slot, sides):
        place = pl.ds(pl.multiple_of(n * depth, depth), depth)
        return [
            pltpu.make_async_copy(terms.at[slot, k], outs[first_out + k].at[:, place, :], out_sems.at[slot, k])
            for k in range(sides * INNER)
        ]

    def work(n, spread, terms, first_out, at, slot, sides):
        for p in range(PLANES):
            pltpu.make_async_copy(own, amp.at[n, p], in_sems.at[n, p]).wait()
        for p in range(PLANES):
            for h, half in enumerate(split_rows(amp[n, p])):
                halves[h, p * size : (p + 1) * size] = half
        parts = [
            jnp.dot(spread[...], halves[h], preferred_element_type=jnp.float32).reshape(-1, HALF, width)
            for h in range(depth // HALF)
        ]
        term = jnp.concatenate(parts, axis=1).astype(jnp.bfloat16)
        terms[slot] = term.reshape(sides * INNER, pair_dev, depth, width)
        for copy in store(terms, first_out, at, slot, sides):
            copy.start()

    @pl.when(middle)
    def _():
        near_spread[:size] = wide_spread[...]
        near_spread[size:] = spread_of(1)

        def one(n, carry):
            work(n, near_spread, near_terms, 0, n, n, 2)
            return carry

        lax.fori_loop(0, narrow_count, one, 0)
        for n in range(narrow_count):
            for copy in store(near_terms, 0, n, n, 2):
                copy.wait()

    def one(n, carry):
        work(n + narrow_count, wide_spread, wide_terms, 2 * INNER, n, n, 1)
        return carry

    lax.fori_loop(0, wide_count, one, 0)
    for n in range(wide_count):
        for copy in store(wide_terms, 2 * INNER, n, n, 1):
            copy.wait()


def ladder_terms(narrow, wide, own, plus, minus, summed, mask, places):
    rows, depth, width = own[wide[0]].shape
    pair_dev = rows // INNER
    arrays, table = [], {z: [] for z in range(PLANES)}
    for chunk in narrow + wide:
        sources = place_sources(own[chunk], plus, minus, chunk)
        for z in range(PLANES):
            numbers = numbered(arrays, [sources[z][p] for p in range(PLANES)]) if z in sources else None
            table[z].append(numbers)
    far = len(arrays)
    operands = arrays + [summed, mask, *places]
    size = rows * HALF
    sems = max(len(narrow), len(wide))
    shapes = [(pair_dev, len(group) * depth, width) for group in (narrow, narrow, wide) for _ in range(INNER)]
    return pl.pallas_call(
        functools.partial(ladder_kernel, table, len(wide), pair_dev),
        out_shape=[jax.ShapeDtypeStruct(shape, jnp.bfloat16) for shape in shapes],
        in_specs=[pl.BlockSpec(memory_space=pl.ANY)] * far
        + [pl.BlockSpec(memory_space=pltpu.VMEM)] * (len(operands) - far),
        out_specs=[pl.BlockSpec(memory_space=pl.ANY)] * len(shapes),
        scratch_shapes=[
            pltpu.VMEM((len(narrow) + len(wide), PLANES, rows, depth, width), jnp.bfloat16),
            pltpu.VMEM((2 * size, PLANES * size), jnp.bfloat16),
            pltpu.VMEM((size, PLANES * size), jnp.bfloat16),
            pltpu.VMEM((depth // HALF, PLANES * size, width), jnp.bfloat16),
            pltpu.VMEM((len(narrow), 2 * INNER, pair_dev, depth, width), jnp.bfloat16),
            pltpu.VMEM((len(wide), INNER, pair_dev, depth, width), jnp.bfloat16),
            pltpu.SemaphoreType.DMA((len(narrow) + len(wide), PLANES)),
            pltpu.SemaphoreType.DMA((sems, 2 * INNER)),
        ],
        compiler_params=pltpu.CompilerParams(vmem_limit_bytes=VMEM_BYTES),
        cost_estimate=pl.CostEstimate(
            flops=2 * PLANES * size * size * width * 2 * (2 * len(narrow) + len(wide)),
            bytes_accessed=(PLANES + 2) * rows * depth * width * 2 * (len(narrow) + len(wide)),
            transcendentals=0,
        ),
        name="ladder",
    )(*operands)


def scale_kernel(flip, first, count, fock_ref, inverse_ref, *refs):
    pieces, (out_ref, fock, inverse, ladder, sems) = refs[:count], refs[count:]
    plane, me = here()
    pair_dev, rows, _ = fock.shape
    start = pl.multiple_of((me ^ flip) * (CHUNK * CHUNKS) + first * CHUNK, CHUNK)
    place = pl.ds(start, rows)

    def load(p):
        return (
            pltpu.make_async_copy(fock_ref.at[p, place], fock.at[p], sems.at[p, 0]),
            pltpu.make_async_copy(inverse_ref.at[p, place], inverse.at[p], sems.at[p, 1]),
        )

    def piece(p, source):
        return pltpu.make_async_copy(source.at[p], ladder.at[p], sems.at[p, 2])

    def store(p):
        return pltpu.make_async_copy(fock.at[p], out_ref.at[p, place], sems.at[p, 3])

    middle = (plane == 1) | (plane == 2)
    for p in range(pair_dev):
        for copy in load(p):
            copy.start()
        if count == 1:
            piece(p, pieces[0]).start()
        else:
            pl.when(middle)(piece(p, pieces[0]).start)
            pl.when(jnp.logical_not(middle))(piece(p, pieces[1]).start)

    def one_pair(p, carry):
        for copy in (*load(p), piece(p, pieces[0])):
            copy.wait()
        total = fock[p].astype(jnp.float32) + ladder[p].astype(jnp.float32)
        fock[p] = (total * inverse[p]).astype(fock.dtype)
        store(p).start()
        return carry

    lax.fori_loop(0, pair_dev, one_pair, 0)
    for p in range(pair_dev):
        store(p).wait()


def add_and_scale(buffer, inverse, pieces, flip, first):
    shape = pieces[0].shape
    size = shape[0] * shape[1] * shape[2]
    return pl.pallas_call(
        functools.partial(scale_kernel, flip, first, len(pieces)),
        out_shape=jax.ShapeDtypeStruct(buffer.shape, buffer.dtype),
        in_specs=[pl.BlockSpec(memory_space=pl.ANY)] * (2 + len(pieces)),
        out_specs=pl.BlockSpec(memory_space=pl.ANY),
        scratch_shapes=[
            pltpu.VMEM(shape, buffer.dtype),
            pltpu.VMEM(shape, jnp.float32),
            pltpu.VMEM(shape, buffer.dtype),
            pltpu.SemaphoreType.DMA((shape[0], 4)),
        ],
        input_output_aliases={0: 0},
        compiler_params=pltpu.CompilerParams(vmem_limit_bytes=VMEM_BYTES),
        cost_estimate=pl.CostEstimate(
            flops=2 * size, bytes_accessed=(8 + 2 * len(pieces)) * size, transcendentals=0
        ),
        name="add_and_scale",
    )(buffer, inverse, *pieces)


def move_kernel(moves, count, *refs):
    outs, sems = refs[count:-1], refs[-1]
    _, me = here()
    copies = []
    for n, (source, flip, at, target, place) in enumerate(moves):
        ref = refs[source]
        if flip is None:
            ref = ref.at[at]
        else:
            start = pl.multiple_of((me ^ flip) * (CHUNK * CHUNKS) + at.start, CHUNK)
            ref = ref.at[:, pl.ds(start, at.stop - at.start), :]
        copies.append(pltpu.make_async_copy(ref, outs[target].at[place], sems.at[n]))
    for copy in copies:
        copy.start()
    for copy in copies:
        copy.wait()


def move(operands, shapes, moves, name):
    moved = 2 * sum(2 * shape[0] * shape[-2] * shape[-1] for shape in shapes)
    call = pl.pallas_call(
        functools.partial(move_kernel, moves, len(operands)),
        out_shape=[jax.ShapeDtypeStruct(shape, jnp.bfloat16) for shape in shapes],
        in_specs=[pl.BlockSpec(memory_space=pl.ANY)] * len(operands),
        out_specs=[pl.BlockSpec(memory_space=pltpu.VMEM)] * len(shapes),
        scratch_shapes=[pltpu.SemaphoreType.DMA((len(moves),))],
        compiler_params=pltpu.CompilerParams(vmem_limit_bytes=VMEM_BYTES),
        cost_estimate=pl.CostEstimate(flops=0, bytes_accessed=moved, transcendentals=0),
        name=name,
    )
    return list(call(*operands))


def rows_of(chunk, first=0):
    return slice((chunk - first) * CHUNK, (chunk - first + 1) * CHUNK)


def core_moves(source, group, target):
    rows = slice(group[0] * CHUNK, group[1] * CHUNK)
    return [(source, 1 + 2 * side, rows, target, (slice(None), side)) for side in range(2)]


def across_moves(source, core, first, group, pair_dev, target):
    rows = slice(group[0] * CHUNK, group[1] * CHUNK)
    near = slice((group[0] - first) * CHUNK, (group[1] - first) * CHUNK)
    return [
        (source, 2, rows, target, slice(0, pair_dev)),
        (core, None, (slice(None), 1, near), target, slice(pair_dev, 2 * pair_dev)),
    ]


def own_moves(source, core, first, across, group, pair_dev, target):
    moves = []
    for n, chunk in enumerate(range(*group)):
        moves += [
            (source, 0, rows_of(chunk), target + n, slice(0, pair_dev)),
            (core, None, (slice(None), 0, rows_of(chunk, first)), target + n, slice(pair_dev, 2 * pair_dev)),
            (across, None, (slice(None), rows_of(chunk, group[0])), target + n, slice(2 * pair_dev, 4 * pair_dev)),
        ]
    return moves


def pick_kernel(choices, *refs):
    outs, sems = refs[-3:-1], refs[-1]
    plane, _ = here()

    def each(do):
        for n, table in enumerate(choices):
            for far, source in table.items():
                at = far if n == 0 else PLANES - 1 - far
                copy = pltpu.make_async_copy(refs[source], outs[n], sems.at[n])
                pl.when(plane == at)(getattr(copy, do))

    each("start")
    each("wait")


def pick(choices, name, after=()):
    arrays = []
    tables = [dict(zip(table, numbered(arrays, table.values()))) for table in choices]
    example = arrays[0]
    arrays += after
    size = example.size
    return pl.pallas_call(
        functools.partial(pick_kernel, tables),
        out_shape=[jax.ShapeDtypeStruct(example.shape, example.dtype)] * 2,
        in_specs=[pl.BlockSpec(memory_space=pl.ANY)] * len(arrays),
        out_specs=[pl.BlockSpec(memory_space=pltpu.VMEM)] * 2,
        scratch_shapes=[pltpu.SemaphoreType.DMA((2,))],
        compiler_params=pltpu.CompilerParams(vmem_limit_bytes=VMEM_BYTES),
        cost_estimate=pl.CostEstimate(flops=0, bytes_accessed=8 * size, transcendentals=0),
        name=name,
    )(*arrays)


def line_round(step, own, int_own, got, after, done_with):
    first, last = 0, 2
    int_first = CHUNKS + 1
    choices = []
    for have in got:
        if step < WIDE:
            table = {far: own[step] for far in range(3)}
        elif step < CHUNKS:
            table = {0: own[step], 1: own[step], 2: have[step - WIDE]}
        else:
            table = {1: have[step - CHUNKS]}
            if int_first <= step < int_first + CHUNKS - WIDE:
                table[0] = int_own[WIDE + step - int_first]
            else:
                first = 1
            if step < 2 * WIDE:
                table[2] = have[step - WIDE]
            elif step < 3 * WIDE:
                table[2] = have[step - 2 * WIDE + CHUNKS]
            else:
                last = 1
        choices.append(table)
    if not after and (step < WIDE or first == last):
        sends = [table[1] for table in choices]
    else:
        sends = done_with(list(pick(choices, f"pick_{step}", after)))
    got[0][step] = lax.ppermute(sends[0], "blk", plane_perm(1, first, last))
    got[1][step] = lax.ppermute(sends[1], "blk", plane_perm(-1, PLANES - 1 - last, PLANES - 1 - first))


def line_exchanges(amplitudes, integrals, hole, beside, beside_later):
    pair_dev, _, width = amplitudes.shape
    rows = INNER * pair_dev
    full = (rows, CHUNK, width)
    own, int_own, got = {}, {}, ({}, {})

    def across_shape(group):
        return (2 * pair_dev, (group[1] - group[0]) * CHUNK, width)

    last = []

    def in_turn(operands):
        return list(operands) + last

    def done_with(found):
        last[:] = found[:1]
        return found

    def arrived(step):
        return [have[step] for have in got]

    def rounds(*steps, after=()):
        for step in steps:
            before = arrived(step - 2) if step >= 2 else []
            line_round(step, own, int_own, got, in_turn(before + list(after)) if step not in (0, 1, 4) else [], done_with)

    groups = ((2, 4), (4, CHUNKS))
    core_first = groups[0][0]
    flips = (2, 3, 1)
    pieces = [
        (0, flip, rows_of(chunk), len(flips) * chunk + n, slice(None))
        for chunk in range(core_first)
        for n, flip in enumerate(flips)
    ]
    def send_across(source, core, first, group):
        (across,) = done_with(
            move(
                in_turn([source, core]),
                [across_shape(group)],
                across_moves(0, 1, first, group, pair_dev, 0),
                f"move_across_{group[0]}",
            )
        )
        return lax.ppermute(across, "blk", inner_perm(2))

    def assemble(source, core, across, first, group, found_in, before=()):
        operands = in_turn([source, core, across] + list(before))
        moves = own_moves(0, 1, first, 2, group, pair_dev, 0)
        found = done_with(move(operands, [full] * (group[1] - group[0]), moves, f"move_own_{group[0]}"))
        found_in.update(zip(range(*group), found))

    def send_core(source, first):
        shape = (pair_dev, 2, (CHUNKS - first) * CHUNK, width)
        (core,) = done_with(move(in_turn([source]), [shape], core_moves(0, (first, CHUNKS), 0), f"move_core_{first}"))
        return lax.ppermute(core, "blk", inner_perm(1))

    int_groups = ((WIDE, CHUNKS), (0, WIDE))
    sent = done_with(move([amplitudes], [(pair_dev, CHUNK, width)] * len(pieces), pieces, "move_first"))
    sent = [lax.ppermute(part, "blk", inner_perm(flips[n % len(flips)])) for n, part in enumerate(sent)]
    core = send_core(amplitudes, core_first)
    for chunk in range(core_first):
        parts = sent[len(flips) * chunk : len(flips) * (chunk + 1)]
        moves = [(0, 0, rows_of(chunk), 0, slice(0, pair_dev))]
        for n, flip in enumerate(flips):
            moves.append((1 + n, None, slice(None), 0, slice(flip * pair_dev, (flip + 1) * pair_dev)))
        (own[chunk],) = done_with(move(in_turn([amplitudes] + parts), [full], moves, "move_own"))
        rounds(chunk)
        if chunk == 0:
            across = send_across(amplitudes, core, core_first, groups[0])
    int_core = send_core(integrals, 0)
    assemble(amplitudes, core, across, core_first, groups[0], own, arrived(0))
    across = send_across(amplitudes, core, core_first, groups[1])
    rounds(2, after=beside)
    rounds(3)
    assemble(amplitudes, core, across, core_first, groups[1], own, arrived(2))
    rounds(4)
    across = send_across(integrals, int_core, 0, int_groups[0])
    rounds(5)
    rounds(6, after=beside_later[1:])
    across_later = send_across(integrals, int_core, 0, int_groups[1])
    rounds(7, after=beside_later[:1])
    rounds(8)
    assemble(integrals, int_core, across, 0, int_groups[0], int_own)

    wide, narrow = tuple(range(WIDE)), tuple(range(WIDE, CHUNKS))
    acc = jnp.zeros((2, PLANES * rows, rows * HALF), jnp.float32)

    def add(*what, acc, **more):
        return done_with([add_pair_sums(*what, own, got, int_own, acc, after=in_turn([]), **more)])[0]

    acc = add(narrow, (0, 1, 2), True, False, acc=acc)
    rounds(9)
    rounds(10)
    assemble(integrals, int_core, across_later, 0, int_groups[1], int_own)
    rounds(11)
    for part in range(3):
        acc = add(wide, (part,), True, False, acc=acc)
        rounds(12 + part)
    acc = add(narrow, (0, 1, 2), False, True, acc=acc)
    rounds(15)
    acc = add(wide[:3], None, True, False, acc=acc)
    acc = add(wide[3:], None, True, False, acc=acc)
    acc = add(narrow[:-1], None, True, True, acc=acc)
    acc = add(narrow[-1:], None, True, True, acc=acc, hole=hole)
    return own, *got, acc


def line_plan(
    amplitudes,
    integrals,
    fock_matrix,
    hole_ladder,
    virt_irrep,
    occ_irrep,
    pair_index,
    eps_occ,
    eps_virt,
):
    pair_dev, virt_rows, virt_all = amplitudes.shape
    pair_total = pair_dev * PLANES * INNER
    blk_id = lax.axis_index("blk")
    rep_id = lax.axis_index("rep")
    plane, me = here()
    half = virt_all // 2
    piece = lax.dynamic_slice_in_dim(fock_matrix, rep_id * half, half, axis=1)
    piece = lax.all_gather(piece, "blk", axis=0, tiled=True)
    fock_all = lax.all_gather(piece, "rep", axis=1, tiled=True)
    kept = jnp.where(virt_irrep[:, None] == virt_irrep[None, :], fock_all, jnp.zeros_like(fock_all))
    fock_term = jnp.einsum(
        "pac,bc->pab", amplitudes, kept, preferred_element_type=jnp.float32
    ).astype(jnp.bfloat16)

    pair_irrep = jnp.bitwise_xor(
        table_lookup(pair_index[:, 0], occ_irrep), table_lookup(pair_index[:, 1], occ_irrep)
    )
    pair_energy = table_lookup(pair_index[:, 0], eps_occ) + table_lookup(pair_index[:, 1], eps_occ)
    mask = (pair_irrep[:, None] == pair_irrep[None, :]).astype(jnp.float32)
    mask = jnp.pad(mask, ((0, 0), (0, LANES - pair_total)))
    own_energy = lax.dynamic_slice_in_dim(pair_energy, blk_id * pair_dev, pair_dev)
    row_energy = lax.dynamic_slice_in_dim(eps_virt, rep_id * virt_rows, virt_rows)
    inverse = 1.0 / (own_energy[:, None, None] - row_energy[None, :, None] - eps_virt[None, None, :])

    hole = jnp.zeros((pair_total, LANES), jnp.float32)
    hole_rows = jnp.pad(hole_ladder, ((0, 0), (0, LANES - pair_total)))
    hole = lax.dynamic_update_slice_in_dim(hole, hole_rows, blk_id * pair_dev, axis=0)
    hole = jnp.where(rep_id == 0, hole, jnp.zeros_like(hole))
    places = ladder_places(pair_dev)
    own, plus, minus, acc = line_exchanges(
        amplitudes, integrals, hole, [piece], [fock_term, inverse, mask, places[2]]
    )
    summed = acc + lax.ppermute(acc, "blk", inner_perm(1))
    count = PLANES * INNER
    for flips in (((1, 0), (0, 2), (1, 2)), ((0, 4), (0, 8), (0, 12))):
        parts = [
            lax.ppermute(
                summed,
                ("rep", "blk"),
                [(r * count + i, (r ^ rep) * count + (i ^ flip)) for r in range(2) for i in range(count)],
            )
            for rep, flip in flips
        ]
        summed = (summed + parts[0]) + (parts[1] + parts[2])
    wide, narrow = tuple(range(WIDE)), tuple(range(WIDE, CHUNKS))
    found = ladder_terms(narrow, wide, own, plus, minus, summed, mask, places)
    outside, inside, every = {}, {}, {}
    for flip in (2, 3, 0, 1):
        inside[flip] = lax.ppermute(found[flip], "blk", inner_perm(flip, (1, 2))) if flip else found[flip]
        outside[flip] = lax.ppermute(found[INNER + flip], "blk", outward_perm(flip))
    for flip in (2, 3, 1, 0):
        term = found[2 * INNER + flip]
        every[flip] = lax.ppermute(term, "blk", inner_perm(flip)) if flip else term
    update = fock_term
    order = ((1, 0), (1, 1), (0, 2), (0, 3), (0, 1), (0, 0), (1, 2), (1, 3))
    for is_wide, flip in order:
        pieces = [every[flip]] if is_wide else [inside[flip], outside[flip]]
        update = add_and_scale(update, inverse, pieces, flip, 0 if is_wide else WIDE)
    return update


def solution(mesh):
    fits = mesh.shape["blk"] == PLANES * INNER and mesh.shape["rep"] == 2
    return jax.shard_map(
        line_plan if fits else spread_plan,
        mesh=mesh,
        in_specs=(
            P("blk", "rep", None),
            P("blk", "rep", None),
            P("blk", None),
            P("blk", None),
            P(),
            P(),
            P(),
            P(),
            P(),
        ),
        out_specs=P("blk", "rep", None),
        check_vma=False,
    )
```

```python
import functools

import jax
import jax.numpy as jnp
from jax import lax
from jax.experimental import pallas as pl
from jax.experimental.pallas import tpu as pltpu
from jax.sharding import PartitionSpec as P

PLANES = 4
INNER = 4
CHUNK = 16
HALF = 8
CHUNKS = 8
WIDE = 5
LANES = 128
VMEM_BYTES = 63 * 1024 * 1024


def table_lookup(index_col, table):
    iota_rows = jnp.arange(table.shape[0], dtype=jnp.int32)
    equal = index_col[:, None] == iota_rows[None, :]
    return jnp.sum(jnp.where(equal, table[None, :], jnp.zeros_like(table)[None, :]), axis=1)


def spread_plan(
    amplitudes,
    integrals,
    fock_matrix,
    hole_ladder,
    virt_irrep,
    occ_irrep,
    pair_index,
    eps_occ,
    eps_virt,
):
    pair_dev = amplitudes.shape[0]
    virt_rows = amplitudes.shape[1]
    virt_all = amplitudes.shape[2]
    blk_count = lax.axis_size("blk")
    rows_each = virt_rows // blk_count
    pair_total = pair_dev * blk_count
    blk_id = lax.axis_index("blk")
    rep_id = lax.axis_index("rep")
    piece = lax.all_gather(fock_matrix, "blk", axis=0, tiled=True)
    kept = jnp.where(virt_irrep[:, None] == virt_irrep[None, :], piece, jnp.zeros_like(piece))
    fock_term = jnp.einsum(
        "pac,bc->pab", amplitudes, kept, preferred_element_type=jnp.float32
    ).astype(jnp.bfloat16)
    amp_virt, int_virt = (
        lax.all_to_all(amplitudes, "blk", split_axis=1, concat_axis=0, tiled=True),
        lax.all_to_all(integrals, "blk", split_axis=1, concat_axis=0, tiled=True),
    )
    amp_flat = amp_virt.reshape(pair_total, rows_each * virt_all)
    int_flat = int_virt.reshape(pair_total, rows_each * virt_all)
    partial_sums = jnp.dot(amp_flat, int_flat.T, preferred_element_type=jnp.float32)
    pair_irrep = jnp.bitwise_xor(
        table_lookup(pair_index[:, 0], occ_irrep), table_lookup(pair_index[:, 1], occ_irrep)
    )
    pair_energy = table_lookup(pair_index[:, 0], eps_occ) + table_lookup(pair_index[:, 1], eps_occ)
    summed = lax.psum(partial_sums, ("rep", "blk"))
    hole_all = lax.all_gather(hole_ladder, "blk", axis=0, tiled=True)
    same_pair = pair_irrep[:, None] == pair_irrep[None, :]
    ladder = jnp.where(same_pair, hole_all + summed, jnp.zeros_like(summed)).astype(jnp.bfloat16)
    ladder_virt = jnp.dot(ladder, amp_flat, preferred_element_type=jnp.float32)
    ladder_virt = ladder_virt.reshape(pair_total, rows_each, virt_all).astype(jnp.bfloat16)
    ladder_term = lax.all_to_all(ladder_virt, "blk", split_axis=0, concat_axis=1, tiled=True)
    row_energy = lax.dynamic_slice_in_dim(eps_virt, rep_id * virt_rows, virt_rows)
    own_energy = lax.dynamic_slice_in_dim(pair_energy, blk_id * pair_dev, pair_dev)
    denom = own_energy[:, None, None] - row_energy[None, :, None] - eps_virt[None, None, :]
    total = fock_term.astype(jnp.float32) + ladder_term.astype(jnp.float32)
    return (total / denom).astype(jnp.bfloat16)


def plane_perm(step, first, last):
    return [
        (plane * INNER + at, (plane + step) * INNER + at)
        for plane in range(first, last + 1)
        for at in range(INNER)
    ]


def inner_perm(flip, planes=range(PLANES)):
    return [(p * INNER + at, p * INNER + (at ^ flip)) for p in planes for at in range(INNER)]


def outward_perm(flip):
    return [
        (p * INNER + at, q * INNER + (at ^ flip)) for p, q in ((1, 0), (2, 3)) for at in range(INNER)
    ]


def sixth(index):
    return sum((index >= edge).astype(jnp.int32) for edge in (6, 12, 18))


def pair_at(index, me, pair_dev):
    group = sixth(index)
    return pair_dev * (me ^ group) + index - pair_dev * group


def place_sources(own, plus, minus, chunk):
    table = {
        1: {0: plus.get(chunk), 1: own, 2: minus.get(chunk), 3: minus.get(CHUNKS + chunk)},
        2: {0: plus.get(CHUNKS + chunk), 1: plus.get(chunk), 2: own, 3: minus.get(chunk)},
    }
    if chunk < WIDE:
        table[0] = {0: own, 1: minus.get(chunk), 2: minus.get(WIDE + chunk), 3: minus.get(2 * WIDE + chunk)}
        table[3] = {0: plus.get(2 * WIDE + chunk), 1: plus.get(WIDE + chunk), 2: plus.get(chunk), 3: own}
    return table


def late_plane(plane):
    return PLANES - 1 if plane < 2 else 0


def numbered(arrays, chosen):
    numbers = []
    for array in chosen:
        found = [n for n, other in enumerate(arrays) if other is array]
        if not found:
            found = [len(arrays)]
            arrays.append(array)
        numbers.append(found[0])
    return numbers


def here():
    blk = lax.axis_index("blk")
    return lax.div(blk, INNER), lax.rem(blk, INNER)


def kept_sum(gram, depth):
    row_id = lax.broadcasted_iota(jnp.int32, gram.shape, 0)
    col_id = lax.broadcasted_iota(jnp.int32, gram.shape, 1)
    same = (row_id & (depth - 1)) == (col_id & (depth - 1))
    return jnp.where(same, gram, 0.0).reshape(-1, depth, gram.shape[1]).sum(axis=1)


def split_rows(block):
    pairs, depth, width = block.shape
    wide = block.astype(jnp.float32).reshape(pairs, depth // HALF, HALF, width)
    return [wide[:, n].reshape(pairs * HALF, width).astype(block.dtype) for n in range(depth // HALF)]


def exact_dot(left, right):
    return jnp.dot(left, right, preferred_element_type=jnp.float32, precision=lax.Precision.HIGHEST)


def pad_rows(array):
    extra = LANES - array.shape[0]
    return jnp.concatenate([array, jnp.zeros((extra, array.shape[1]), array.dtype)], axis=0)


def pair_kernel(table, near_too, own_too, parts, late, last, pair_dev, *refs):
    acc_in, out_ref, amp, ints, turned, total, sems = refs[-7:]
    plane, me = here()
    chunks, _, rows, depth, width = amp.shape
    sides = ints.shape[1]
    total[...] = acc_in[...]
    for z, (amp_from, int_from) in table.items():

        @pl.when(plane == z)
        def _():
            for c in range(chunks):
                for n in range(sides):
                    pltpu.make_async_copy(refs[int_from[c][n]], ints.at[c, n], sems.at[c, len(parts) + n]).start()
                for n in range(len(parts)):
                    pltpu.make_async_copy(refs[amp_from[c][n]], amp.at[c, n], sems.at[c, n]).start()

    def add_all():
        for c in range(chunks):
            for n in range(sides):
                pltpu.make_async_copy(refs[0], ints.at[c, n], sems.at[c, len(parts) + n]).wait()
                for h, half in enumerate(split_rows(ints[c, n])):
                    turned[c, h, n * rows * HALF : (n + 1) * rows * HALF] = half
            for n in range(len(parts)):
                pltpu.make_async_copy(refs[0], amp.at[c, n], sems.at[c, n]).wait()

        def add_part(n, carry):
            if late:
                p = jnp.where(plane < 2, PLANES - 1, 0)
            else:
                p = jnp.where(plane < 2, n + parts[0], n + parts[0] + 1)
            place = pl.ds(pl.multiple_of(p * rows, 8), rows)
            gram = jnp.zeros((rows * HALF, sides * rows * HALF), jnp.float32)
            for c in range(chunks):
                for h, half in enumerate(split_rows(amp[c, n])):
                    gram += lax.dot_general(
                        half, turned[c, h], (((1,), (1,)), ((), ())), preferred_element_type=jnp.float32
                    )
            for side in range(sides):
                kept = kept_sum(gram[:, side * rows * HALF : (side + 1) * rows * HALF], HALF)
                total[side + (0 if own_too else 1), place] += kept
            return carry

        lax.fori_loop(0, len(parts), add_part, 0)

    if len(table) == PLANES:
        add_all()
    else:
        pl.when((plane == 1) | (plane == 2))(add_all)
    if not last:
        out_ref[...] = total[...]
        return
    hole_ref = refs[-8]
    lanes = total.shape[2]
    summed = jnp.zeros((total.shape[1], LANES), jnp.float32)
    near = jnp.where(plane < 2, 0, PLANES - 1)
    row_id = lax.broadcasted_iota(jnp.int32, (lanes, LANES), 0) // HALF
    col_id = lax.broadcasted_iota(jnp.int32, (lanes, LANES), 1)
    pair_id = pair_at(row_id, me, pair_dev)
    for side, at in ((0, plane), (1, near)):
        chosen = (col_id == pair_id + at * rows).astype(jnp.float32)
        summed += exact_dot(total[side], chosen)
    out_id = lax.broadcasted_iota(jnp.int32, (total.shape[1], LANES), 0)
    in_id = lax.broadcasted_iota(jnp.int32, (total.shape[1], LANES), 1)
    in_plane = sum((in_id >= p * rows).astype(jnp.int32) for p in range(1, PLANES))
    in_pair = pair_at(in_id - in_plane * rows, me, pair_dev) + in_plane * rows
    chosen = (out_id == in_pair).astype(jnp.float32)
    out_ref[...] = hole_ref[...] + exact_dot(chosen, pad_rows(summed))


def add_pair_sums(chunks, parts, own_too, near_too, own, got, int_own, acc, hole=None, after=()):
    late, last = parts is None, hole is not None
    parts = (0,) if late else parts
    rows, depth, width = own[chunks[0]].shape
    arrays, table = [], {}
    for chunk in chunks:
        for z, sources in place_sources(own[chunk], got[0], got[1], chunk).items():
            early = [sources[p] for p in range(PLANES) if p != late_plane(z)]
            amp_from = [sources[late_plane(z)]] if late else [early[n] for n in parts]
            int_from = [int_own[chunk]] if own_too else []
            if near_too:
                int_from.append(got[z - 1][CHUNKS + 1 + chunk - WIDE])
            entry = table.setdefault(z, ([], []))
            entry[0].append(numbered(arrays, amp_from))
            entry[1].append(numbered(arrays, int_from))
    sides = own_too + near_too
    operands = arrays + list(after)
    far = len(operands)
    if last:
        operands.append(hole)
    operands.append(acc)
    shape = (PLANES * rows, LANES) if last else acc.shape
    block = rows * depth
    return pl.pallas_call(
        functools.partial(pair_kernel, table, near_too, own_too, parts, late, last, rows // INNER),
        out_shape=jax.ShapeDtypeStruct(shape, jnp.float32),
        in_specs=[pl.BlockSpec(memory_space=pl.ANY)] * far
        + [pl.BlockSpec(memory_space=pltpu.VMEM)] * (len(operands) - far),
        out_specs=pl.BlockSpec(memory_space=pltpu.VMEM),
        scratch_shapes=[
            pltpu.VMEM((len(chunks), len(parts), rows, depth, width), jnp.bfloat16),
            pltpu.VMEM((len(chunks), sides, rows, depth, width), jnp.bfloat16),
            pltpu.VMEM((len(chunks), depth // HALF, sides * rows * HALF, width), jnp.bfloat16),
            pltpu.VMEM(acc.shape, jnp.float32),
            pltpu.SemaphoreType.DMA((len(chunks), len(parts) + sides)),
        ],
        compiler_params=pltpu.CompilerParams(vmem_limit_bytes=VMEM_BYTES),
        cost_estimate=pl.CostEstimate(
            flops=2 * len(chunks) * len(parts) * sides * block**2 * width,
            bytes_accessed=len(chunks) * (len(parts) + sides) * block * width * 2,
            transcendentals=0,
        ),
        name=f"pair_sums_{chunks[0]}_{'late' if late else parts[0]}",
    )(*operands)


def places_kernel(pair_dev, col_ref, row_ref, keep_ref):
    plane, me = here()
    rows, depth = INNER * pair_dev, HALF
    block = rows * depth
    col = lax.broadcasted_iota(jnp.int32, (LANES, PLANES * block), 1) // depth
    col_plane = sum((col >= p * rows).astype(jnp.int32) for p in range(1, PLANES))
    col_pair = pair_at(col - col_plane * rows, me, pair_dev) + col_plane * rows
    col_ref[...] = (lax.broadcasted_iota(jnp.int32, col.shape, 0) == col_pair).astype(jnp.bfloat16)
    row = lax.broadcasted_iota(jnp.int32, (block, LANES), 0) // depth
    row_pair = pair_at(row, me, pair_dev)
    for side, at in enumerate((plane, jnp.where(plane < 2, 0, PLANES - 1))):
        chosen = lax.broadcasted_iota(jnp.int32, row.shape, 1) == row_pair + at * rows
        row_ref[side] = chosen.astype(jnp.bfloat16)
    left = lax.broadcasted_iota(jnp.int32, (block, PLANES * block), 0) & (depth - 1)
    right = lax.broadcasted_iota(jnp.int32, (block, PLANES * block), 1) & (depth - 1)
    keep_ref[...] = (left == right).astype(jnp.bfloat16)


def ladder_places(pair_dev):
    block = INNER * pair_dev * HALF
    shapes = [(LANES, PLANES * block), (2, block, LANES), (block, PLANES * block)]
    return pl.pallas_call(
        functools.partial(places_kernel, pair_dev),
        out_shape=[jax.ShapeDtypeStruct(shape, jnp.bfloat16) for shape in shapes],
        out_specs=[pl.BlockSpec(memory_space=pltpu.VMEM)] * 3,
        compiler_params=pltpu.CompilerParams(vmem_limit_bytes=VMEM_BYTES),
        name="ladder_places",
    )()


def ladder_kernel(table_of, wide_count, pair_dev, *refs):
    own = refs[0]
    outs = refs[-8 - 3 * INNER : -8]
    sum_ref, mask_ref, col_ref, row_ref, keep_ref = refs[-13 - 3 * INNER : -8 - 3 * INNER]
    amp, near_spread, wide_spread, halves, near_terms, wide_terms, in_sems, out_sems = refs[-8:]
    chunks, _, rows, depth, width = amp.shape
    narrow_count = chunks - wide_count
    plane, _ = here()
    middle = (plane == 1) | (plane == 2)
    for z, table in table_of.items():

        @pl.when(plane == z)
        def _():
            for n, sources in enumerate(table):
                if sources is not None:
                    for p in range(PLANES):
                        pltpu.make_async_copy(refs[sources[p]], amp.at[n, p], in_sems.at[n, p]).start()

    ladder = jnp.where(mask_ref[...] > 0, sum_ref[...], 0.0).astype(jnp.bfloat16)
    ladder = pad_rows(ladder)

    def spread_of(side):
        picked = jnp.dot(row_ref[side], ladder, preferred_element_type=jnp.float32).astype(jnp.bfloat16)
        full = jnp.dot(picked, col_ref[...], preferred_element_type=jnp.float32).astype(jnp.bfloat16)
        return jnp.where(keep_ref[...] > 0, full, jnp.zeros_like(full))

    size = rows * HALF
    wide_spread[...] = spread_of(0)

    def store(terms, first_out, n, slot, sides):
        place = pl.ds(pl.multiple_of(n * depth, depth), depth)
        return [
            pltpu.make_async_copy(terms.at[slot, k], outs[first_out + k].at[:, place, :], out_sems.at[slot, k])
            for k in range(sides * INNER)
        ]

    def work(n, spread, terms, first_out, at, slot, sides):
        for p in range(PLANES):
            pltpu.make_async_copy(own, amp.at[n, p], in_sems.at[n, p]).wait()
        for p in range(PLANES):
            for h, half in enumerate(split_rows(amp[n, p])):
                halves[h, p * size : (p + 1) * size] = half
        parts = [
            jnp.dot(spread[...], halves[h], preferred_element_type=jnp.float32).reshape(-1, HALF, width)
            for h in range(depth // HALF)
        ]
        term = jnp.concatenate(parts, axis=1).astype(jnp.bfloat16)
        terms[slot] = term.reshape(sides * INNER, pair_dev, depth, width)
        for copy in store(terms, first_out, at, slot, sides):
            copy.start()

    @pl.when(middle)
    def _():
        near_spread[:size] = wide_spread[...]
        near_spread[size:] = spread_of(1)

        def one(n, carry):
            work(n, near_spread, near_terms, 0, n, n, 2)
            return carry

        lax.fori_loop(0, narrow_count, one, 0)
        for n in range(narrow_count):
            for copy in store(near_terms, 0, n, n, 2):
                copy.wait()

    def one(n, carry):
        work(n + narrow_count, wide_spread, wide_terms, 2 * INNER, n, n, 1)
        return carry

    lax.fori_loop(0, wide_count, one, 0)
    for n in range(wide_count):
        for copy in store(wide_terms, 2 * INNER, n, n, 1):
            copy.wait()


def ladder_terms(narrow, wide, own, plus, minus, summed, mask, places):
    rows, depth, width = own[wide[0]].shape
    pair_dev = rows // INNER
    arrays, table = [], {z: [] for z in range(PLANES)}
    for chunk in narrow + wide:
        sources = place_sources(own[chunk], plus, minus, chunk)
        for z in range(PLANES):
            numbers = numbered(arrays, [sources[z][p] for p in range(PLANES)]) if z in sources else None
            table[z].append(numbers)
    far = len(arrays)
    operands = arrays + [summed, mask, *places]
    size = rows * HALF
    sems = max(len(narrow), len(wide))
    shapes = [(pair_dev, len(group) * depth, width) for group in (narrow, narrow, wide) for _ in range(INNER)]
    return pl.pallas_call(
        functools.partial(ladder_kernel, table, len(wide), pair_dev),
        out_shape=[jax.ShapeDtypeStruct(shape, jnp.bfloat16) for shape in shapes],
        in_specs=[pl.BlockSpec(memory_space=pl.ANY)] * far
        + [pl.BlockSpec(memory_space=pltpu.VMEM)] * (len(operands) - far),
        out_specs=[pl.BlockSpec(memory_space=pl.ANY)] * len(shapes),
        scratch_shapes=[
            pltpu.VMEM((len(narrow) + len(wide), PLANES, rows, depth, width), jnp.bfloat16),
            pltpu.VMEM((2 * size, PLANES * size), jnp.bfloat16),
            pltpu.VMEM((size, PLANES * size), jnp.bfloat16),
            pltpu.VMEM((depth // HALF, PLANES * size, width), jnp.bfloat16),
            pltpu.VMEM((len(narrow), 2 * INNER, pair_dev, depth, width), jnp.bfloat16),
            pltpu.VMEM((len(wide), INNER, pair_dev, depth, width), jnp.bfloat16),
            pltpu.SemaphoreType.DMA((len(narrow) + len(wide), PLANES)),
            pltpu.SemaphoreType.DMA((sems, 2 * INNER)),
        ],
        compiler_params=pltpu.CompilerParams(vmem_limit_bytes=VMEM_BYTES),
        cost_estimate=pl.CostEstimate(
            flops=2 * PLANES * size * size * width * 2 * (2 * len(narrow) + len(wide)),
            bytes_accessed=(PLANES + 2) * rows * depth * width * 2 * (len(narrow) + len(wide)),
            transcendentals=0,
        ),
        name="ladder",
    )(*operands)


def scale_kernel(flip, first, count, fock_ref, inverse_ref, *refs):
    pieces, (out_ref, fock, inverse, ladder, sems) = refs[:count], refs[count:]
    plane, me = here()
    pair_dev, rows, _ = fock.shape
    start = pl.multiple_of((me ^ flip) * (CHUNK * CHUNKS) + first * CHUNK, CHUNK)
    place = pl.ds(start, rows)

    def load(p):
        return (
            pltpu.make_async_copy(fock_ref.at[p, place], fock.at[p], sems.at[p, 0]),
            pltpu.make_async_copy(inverse_ref.at[p, place], inverse.at[p], sems.at[p, 1]),
        )

    def piece(p, source):
        return pltpu.make_async_copy(source.at[p], ladder.at[p], sems.at[p, 2])

    def store(p):
        return pltpu.make_async_copy(fock.at[p], out_ref.at[p, place], sems.at[p, 3])

    middle = (plane == 1) | (plane == 2)
    for p in range(pair_dev):
        for copy in load(p):
            copy.start()
        if count == 1:
            piece(p, pieces[0]).start()
        else:
            pl.when(middle)(piece(p, pieces[0]).start)
            pl.when(jnp.logical_not(middle))(piece(p, pieces[1]).start)

    def one_pair(p, carry):
        for copy in (*load(p), piece(p, pieces[0])):
            copy.wait()
        total = fock[p].astype(jnp.float32) + ladder[p].astype(jnp.float32)
        fock[p] = (total * inverse[p]).astype(fock.dtype)
        store(p).start()
        return carry

    lax.fori_loop(0, pair_dev, one_pair, 0)
    for p in range(pair_dev):
        store(p).wait()


def add_and_scale(buffer, inverse, pieces, flip, first):
    shape = pieces[0].shape
    size = shape[0] * shape[1] * shape[2]
    return pl.pallas_call(
        functools.partial(scale_kernel, flip, first, len(pieces)),
        out_shape=jax.ShapeDtypeStruct(buffer.shape, buffer.dtype),
        in_specs=[pl.BlockSpec(memory_space=pl.ANY)] * (2 + len(pieces)),
        out_specs=pl.BlockSpec(memory_space=pl.ANY),
        scratch_shapes=[
            pltpu.VMEM(shape, buffer.dtype),
            pltpu.VMEM(shape, jnp.float32),
            pltpu.VMEM(shape, buffer.dtype),
            pltpu.SemaphoreType.DMA((shape[0], 4)),
        ],
        input_output_aliases={0: 0},
        compiler_params=pltpu.CompilerParams(vmem_limit_bytes=VMEM_BYTES),
        cost_estimate=pl.CostEstimate(
            flops=2 * size, bytes_accessed=(8 + 2 * len(pieces)) * size, transcendentals=0
        ),
        name="add_and_scale",
    )(buffer, inverse, *pieces)


def move_kernel(moves, count, *refs):
    outs, sems = refs[count:-1], refs[-1]
    _, me = here()
    copies = []
    for n, (source, flip, at, target, place) in enumerate(moves):
        ref = refs[source]
        if flip is None:
            ref = ref.at[at]
        else:
            start = pl.multiple_of((me ^ flip) * (CHUNK * CHUNKS) + at.start, CHUNK)
            ref = ref.at[:, pl.ds(start, at.stop - at.start), :]
        copies.append(pltpu.make_async_copy(ref, outs[target].at[place], sems.at[n]))
    for copy in copies:
        copy.start()
    for copy in copies:
        copy.wait()


def move(operands, shapes, moves, name):
    moved = 2 * sum(2 * shape[0] * shape[-2] * shape[-1] for shape in shapes)
    call = pl.pallas_call(
        functools.partial(move_kernel, moves, len(operands)),
        out_shape=[jax.ShapeDtypeStruct(shape, jnp.bfloat16) for shape in shapes],
        in_specs=[pl.BlockSpec(memory_space=pl.ANY)] * len(operands),
        out_specs=[pl.BlockSpec(memory_space=pltpu.VMEM)] * len(shapes),
        scratch_shapes=[pltpu.SemaphoreType.DMA((len(moves),))],
        compiler_params=pltpu.CompilerParams(vmem_limit_bytes=VMEM_BYTES),
        cost_estimate=pl.CostEstimate(flops=0, bytes_accessed=moved, transcendentals=0),
        name=name,
    )
    return list(call(*operands))


def rows_of(chunk, first=0):
    return slice((chunk - first) * CHUNK, (chunk - first + 1) * CHUNK)


def core_moves(source, group, target):
    rows = slice(group[0] * CHUNK, group[1] * CHUNK)
    return [(source, 1 + 2 * side, rows, target, (slice(None), side)) for side in range(2)]


def across_moves(source, core, first, group, pair_dev, target):
    rows = slice(group[0] * CHUNK, group[1] * CHUNK)
    near = slice((group[0] - first) * CHUNK, (group[1] - first) * CHUNK)
    return [
        (source, 2, rows, target, slice(0, pair_dev)),
        (core, None, (slice(None), 1, near), target, slice(pair_dev, 2 * pair_dev)),
    ]


def own_moves(source, core, first, across, group, pair_dev, target):
    moves = []
    for n, chunk in enumerate(range(*group)):
        moves += [
            (source, 0, rows_of(chunk), target + n, slice(0, pair_dev)),
            (core, None, (slice(None), 0, rows_of(chunk, first)), target + n, slice(pair_dev, 2 * pair_dev)),
            (across, None, (slice(None), rows_of(chunk, group[0])), target + n, slice(2 * pair_dev, 4 * pair_dev)),
        ]
    return moves


def pick_kernel(choices, *refs):
    outs, sems = refs[-3:-1], refs[-1]
    plane, _ = here()

    def each(do):
        for n, table in enumerate(choices):
            for far, source in table.items():
                at = far if n == 0 else PLANES - 1 - far
                copy = pltpu.make_async_copy(refs[source], outs[n], sems.at[n])
                pl.when(plane == at)(getattr(copy, do))

    each("start")
    each("wait")


def pick(choices, name, after=()):
    arrays = []
    tables = [dict(zip(table, numbered(arrays, table.values()))) for table in choices]
    example = arrays[0]
    arrays += after
    size = example.size
    return pl.pallas_call(
        functools.partial(pick_kernel, tables),
        out_shape=[jax.ShapeDtypeStruct(example.shape, example.dtype)] * 2,
        in_specs=[pl.BlockSpec(memory_space=pl.ANY)] * len(arrays),
        out_specs=[pl.BlockSpec(memory_space=pltpu.VMEM)] * 2,
        scratch_shapes=[pltpu.SemaphoreType.DMA((2,))],
        compiler_params=pltpu.CompilerParams(vmem_limit_bytes=VMEM_BYTES),
        cost_estimate=pl.CostEstimate(flops=0, bytes_accessed=8 * size, transcendentals=0),
        name=name,
    )(*arrays)


def line_round(step, own, int_own, got, after, done_with):
    first, last = 0, 2
    int_first = CHUNKS + 1
    choices = []
    for have in got:
        if step < WIDE:
            table = {far: own[step] for far in range(3)}
        elif step < CHUNKS:
            table = {0: own[step], 1: own[step], 2: have[step - WIDE]}
        else:
            table = {1: have[step - CHUNKS]}
            if int_first <= step < int_first + CHUNKS - WIDE:
                table[0] = int_own[WIDE + step - int_first]
            else:
                first = 1
            if step < 2 * WIDE:
                table[2] = have[step - WIDE]
            elif step < 3 * WIDE:
                table[2] = have[step - 2 * WIDE + CHUNKS]
            else:
                last = 1
        choices.append(table)
    if not after and (step < WIDE or first == last):
        sends = [table[1] for table in choices]
    else:
        sends = done_with(list(pick(choices, f"pick_{step}", after)))
    got[0][step] = lax.ppermute(sends[0], "blk", plane_perm(1, first, last))
    got[1][step] = lax.ppermute(sends[1], "blk", plane_perm(-1, PLANES - 1 - last, PLANES - 1 - first))


def line_exchanges(amplitudes, integrals, hole, beside, beside_later):
    pair_dev, _, width = amplitudes.shape
    rows = INNER * pair_dev
    full = (rows, CHUNK, width)
    own, int_own, got = {}, {}, ({}, {})

    def across_shape(group):
        return (2 * pair_dev, (group[1] - group[0]) * CHUNK, width)

    last = []

    def in_turn(operands):
        return list(operands) + last

    def done_with(found):
        last[:] = found[:1]
        return found

    def arrived(step):
        return [have[step] for have in got]

    def rounds(*steps, after=()):
        for step in steps:
            before = arrived(step - 2) if step >= 2 else []
            line_round(step, own, int_own, got, in_turn(before + list(after)) if step not in (0, 1, 4) else [], done_with)

    groups = ((2, 4), (4, CHUNKS))
    core_first = groups[0][0]
    flips = (2, 3, 1)
    pieces = [
        (0, flip, rows_of(chunk), len(flips) * chunk + n, slice(None))
        for chunk in range(core_first)
        for n, flip in enumerate(flips)
    ]
    def send_across(source, core, first, group):
        (across,) = done_with(
            move(
                in_turn([source, core]),
                [across_shape(group)],
                across_moves(0, 1, first, group, pair_dev, 0),
                f"move_across_{group[0]}",
            )
        )
        return lax.ppermute(across, "blk", inner_perm(2))

    def assemble(source, core, across, first, group, found_in, before=()):
        operands = in_turn([source, core, across] + list(before))
        moves = own_moves(0, 1, first, 2, group, pair_dev, 0)
        found = done_with(move(operands, [full] * (group[1] - group[0]), moves, f"move_own_{group[0]}"))
        found_in.update(zip(range(*group), found))

    def send_core(source, first, after=()):
        shape = (pair_dev, 2, (CHUNKS - first) * CHUNK, width)
        (core,) = done_with(move(in_turn([source, *after]), [shape], core_moves(0, (first, CHUNKS), 0), f"move_core_{first}"))
        return lax.ppermute(core, "blk", inner_perm(1))

    int_groups = ((WIDE, CHUNKS), (0, WIDE))
    sent = done_with(move([amplitudes], [(pair_dev, CHUNK, width)] * len(pieces), pieces, "move_first"))
    sent = [lax.ppermute(part, "blk", inner_perm(flips[n % len(flips)])) for n, part in enumerate(sent)]
    core = send_core(amplitudes, core_first, sent[2:3])
    int_core = send_core(integrals, 0)

    def first_chunk(chunk):
        parts = sent[len(flips) * chunk : len(flips) * (chunk + 1)]
        moves = [(0, 0, rows_of(chunk), 0, slice(0, pair_dev))]
        for n, flip in enumerate(flips):
            moves.append((1 + n, None, slice(None), 0, slice(flip * pair_dev, (flip + 1) * pair_dev)))
        (own[chunk],) = done_with(move(in_turn([amplitudes] + parts), [full], moves, "move_own"))
        rounds(chunk)

    first_chunk(0)
    packed = done_with(
        move(
            in_turn([amplitudes, core] + sent[len(flips) : len(flips) + 2]),
            [across_shape(group) for group in groups],
            [one for n, group in enumerate(groups) for one in across_moves(0, 1, core_first, group, pair_dev, n)],
            "move_across",
        )
    )
    acrosses = [lax.ppermute(part, "blk", inner_perm(2)) for part in packed]
    first_chunk(1)
    across = acrosses[0]
    assemble(amplitudes, core, across, core_first, groups[0], own, arrived(0))
    across = acrosses[1]
    rounds(2, after=beside)
    rounds(3)
    assemble(amplitudes, core, across, core_first, groups[1], own, arrived(2))
    rounds(4)
    across = send_across(integrals, int_core, 0, int_groups[0])
    rounds(5)
    rounds(6, after=beside_later[1:])
    across_later = send_across(integrals, int_core, 0, int_groups[1])
    rounds(7, after=beside_later[:1])
    rounds(8)
    assemble(integrals, int_core, across, 0, int_groups[0], int_own)

    wide, narrow = tuple(range(WIDE)), tuple(range(WIDE, CHUNKS))
    acc = jnp.zeros((2, PLANES * rows, rows * HALF), jnp.float32)

    def add(*what, acc, **more):
        return done_with([add_pair_sums(*what, own, got, int_own, acc, after=in_turn([]), **more)])[0]

    acc = add(narrow, (0, 1, 2), True, False, acc=acc)
    rounds(9)
    rounds(10)
    assemble(integrals, int_core, across_later, 0, int_groups[1], int_own)
    rounds(11)
    for part in range(3):
        acc = add(wide, (part,), True, False, acc=acc)
        rounds(12 + part)
    acc = add(narrow, (0, 1, 2), False, True, acc=acc)
    rounds(15)
    acc = add(wide[:3], None, True, False, acc=acc)
    acc = add(wide[3:], None, True, False, acc=acc)
    acc = add(narrow[:-1], None, True, True, acc=acc)
    acc = add(narrow[-1:], None, True, True, acc=acc, hole=hole)
    return own, *got, acc


def line_plan(
    amplitudes,
    integrals,
    fock_matrix,
    hole_ladder,
    virt_irrep,
    occ_irrep,
    pair_index,
    eps_occ,
    eps_virt,
):
    pair_dev, virt_rows, virt_all = amplitudes.shape
    pair_total = pair_dev * PLANES * INNER
    blk_id = lax.axis_index("blk")
    rep_id = lax.axis_index("rep")
    plane, me = here()
    half = virt_all // 2
    piece = lax.dynamic_slice_in_dim(fock_matrix, rep_id * half, half, axis=1)
    piece = lax.all_gather(piece, "blk", axis=0, tiled=True)
    fock_all = lax.all_gather(piece, "rep", axis=1, tiled=True)
    kept = jnp.where(virt_irrep[:, None] == virt_irrep[None, :], fock_all, jnp.zeros_like(fock_all))
    fock_term = jnp.einsum(
        "pac,bc->pab", amplitudes, kept, preferred_element_type=jnp.float32
    ).astype(jnp.bfloat16)

    pair_irrep = jnp.bitwise_xor(
        table_lookup(pair_index[:, 0], occ_irrep), table_lookup(pair_index[:, 1], occ_irrep)
    )
    pair_energy = table_lookup(pair_index[:, 0], eps_occ) + table_lookup(pair_index[:, 1], eps_occ)
    mask = (pair_irrep[:, None] == pair_irrep[None, :]).astype(jnp.float32)
    mask = jnp.pad(mask, ((0, 0), (0, LANES - pair_total)))
    own_energy = lax.dynamic_slice_in_dim(pair_energy, blk_id * pair_dev, pair_dev)
    row_energy = lax.dynamic_slice_in_dim(eps_virt, rep_id * virt_rows, virt_rows)
    inverse = 1.0 / (own_energy[:, None, None] - row_energy[None, :, None] - eps_virt[None, None, :])

    hole = jnp.zeros((pair_total, LANES), jnp.float32)
    hole_rows = jnp.pad(hole_ladder, ((0, 0), (0, LANES - pair_total)))
    hole = lax.dynamic_update_slice_in_dim(hole, hole_rows, blk_id * pair_dev, axis=0)
    hole = jnp.where(rep_id == 0, hole, jnp.zeros_like(hole))
    places = ladder_places(pair_dev)
    own, plus, minus, acc = line_exchanges(
        amplitudes, integrals, hole, [piece], [fock_term, inverse, mask, places[2]]
    )
    summed = acc + lax.ppermute(acc, "blk", inner_perm(1))
    count = PLANES * INNER
    for flips in (((1, 0), (0, 2), (1, 2)), ((0, 4), (0, 8), (0, 12))):
        parts = [
            lax.ppermute(
                summed,
                ("rep", "blk"),
                [(r * count + i, (r ^ rep) * count + (i ^ flip)) for r in range(2) for i in range(count)],
            )
            for rep, flip in flips
        ]
        summed = (summed + parts[0]) + (parts[1] + parts[2])
    wide, narrow = tuple(range(WIDE)), tuple(range(WIDE, CHUNKS))
    found = ladder_terms(narrow, wide, own, plus, minus, summed, mask, places)
    outside, inside, every = {}, {}, {}
    for flip in (2, 3, 0, 1):
        inside[flip] = lax.ppermute(found[flip], "blk", inner_perm(flip, (1, 2))) if flip else found[flip]
        outside[flip] = lax.ppermute(found[INNER + flip], "blk", outward_perm(flip))
    for flip in (2, 3, 1, 0):
        term = found[2 * INNER + flip]
        every[flip] = lax.ppermute(term, "blk", inner_perm(flip)) if flip else term
    update = fock_term
    order = ((1, 0), (1, 1), (0, 2), (0, 3), (0, 1), (0, 0), (1, 2), (1, 3))
    for is_wide, flip in order:
        pieces = [every[flip]] if is_wide else [inside[flip], outside[flip]]
        update = add_and_scale(update, inverse, pieces, flip, 0 if is_wide else WIDE)
    return update


def solution(mesh):
    fits = mesh.shape["blk"] == PLANES * INNER and mesh.shape["rep"] == 2
    return jax.shard_map(
        line_plan if fits else spread_plan,
        mesh=mesh,
        in_specs=(
            P("blk", "rep", None),
            P("blk", "rep", None),
            P("blk", None),
            P("blk", None),
            P(),
            P(),
            P(),
            P(),
            P(),
        ),
        out_specs=P("blk", "rep", None),
        check_vma=False,
    )
```
